512 devices in a mesh: row: 32 (over z_lo, y, core), col: 16 (over x, z_hi).
Axes of the slice: x: 4, y: 8, z: 8 (z_hi: 4, z_lo: 2; z = z_hi * 2 + z_lo), core: 2. Of those that a mesh axis runs over, the one named last changes fastest.
Arguments:
- out_inverse: bfloat16 [14336, 14336], P('row', 'col'), may hold values from -1 to 2, as said below
- gradient: bfloat16 [14336, 4096], P('col', 'row'), may hold values from -6 to 6
- in_inverse: bfloat16 [4096, 4096], P('row', 'col'), may hold values from -1 to 2, as said below
Outputs:
- preconditioned: bfloat16 [14336, 4096], P('row', 'col')
The draws below stay inside these ranges and needn't reach their ends.
Inputs may be any that keep to these rules, and one draw needn't show every extreme that they name: out_inverse is symmetric and positive definite. in_inverse is symmetric and positive definite.
All inputs are finite; a program needn't handle non-finite values.
Results may differ from the reference program's by a relative error of at most 0.02.
Values may be sent and summed in bfloat16 or wider, within the bound.
A program may use at most 64 MiB of HBM per device.

```python
import math
import jax
import jax.numpy as jnp
from jax import lax

D = 4096
FF = 14336
N_COL = 16


def assemble(raw, diag_values):
    order = raw.shape[0]
    sym = (raw + raw.T) * 0.70710678
    rows = lax.broadcasted_iota(jnp.int32, (order, order), 0)
    cols = lax.broadcasted_iota(jnp.int32, (order, order), 1)
    return jnp.where(rows == cols, diag_values[:, None], sym)


def draw_out_inverse(key, part):
    key = jax.random.fold_in(key, 11)
    first, second = jax.random.split(key)
    raw = jax.random.normal(first, (FF, FF), jnp.float32) * (0.35 / math.sqrt(FF))
    diag_values = jax.random.uniform(second, (FF,), jnp.float32, 0.9, 1.6)
    return assemble(raw, diag_values).astype(jnp.bfloat16)


def draw_in_inverse(key, part):
    key = jax.random.fold_in(key, 23)
    first, second = jax.random.split(key)
    raw = jax.random.normal(first, (D, D), jnp.float32) * (0.35 / math.sqrt(D))
    diag_values = jax.random.uniform(second, (D,), jnp.float32, 0.9, 1.6)
    return assemble(raw, diag_values).astype(jnp.bfloat16)


def steps_of(key, shape, cuts, least, largest):
    def one(axis_at, blocks):
        steps = jax.random.uniform(jax.random.fold_in(jax.random.fold_in(key, 6), axis_at), (blocks,), jnp.float32, least / len(cuts), largest / len(cuts))
        return jnp.repeat(jnp.exp(steps), shape[axis_at] // blocks).reshape((-1,) + (1,) * (len(shape) - axis_at - 1))

    loudness = one(*cuts[0])
    for cut in cuts[1:]:
        loudness = loudness * one(*cut)
    return loudness


def normal_values(stream_key, dims, width, most, cuts=(), kind=jnp.bfloat16):
    array = jax.random.normal(stream_key, dims, jnp.float32) * width
    if len(cuts) > 0:
        array = steps_of(stream_key, dims, cuts, -0.22, 0.18) * array
    return jnp.clip(array, min=-most, max=most).astype(kind)


def setup_inputs(seed: int = 0) -> dict:
    streams_of = jax.random.split(jax.random.key(seed), 4)
    return {
        "out_inverse": draw_out_inverse(jax.random.fold_in(streams_of[3], 71), 0),
        "gradient": normal_values(streams_of[1], (FF, D), 1.0, 6.0, ((0, 16), (1, 32))),
        "in_inverse": draw_in_inverse(jax.random.fold_in(streams_of[3], 71), 0),
    }


def reference(out_inverse, gradient, in_inverse):
    span = FF // N_COL

    def add_range(index, total):
        start = (index * span).astype(jnp.int32)
        factor_cols = lax.dynamic_slice_in_dim(out_inverse, start, span, 1)
        grad_part = lax.dynamic_slice_in_dim(gradient, start, span, 0)
        rounded = jnp.dot(factor_cols, grad_part, preferred_element_type=jnp.float32).astype(jnp.bfloat16)
        rounded = lax.optimization_barrier(rounded)
        return total + rounded.astype(jnp.float32)

    total = lax.fori_loop(jnp.int32(0), jnp.int32(N_COL), add_range, jnp.zeros((FF, D), jnp.float32))
    left = total.astype(jnp.bfloat16)
    return jnp.dot(left, in_inverse, preferred_element_type=jnp.float32).astype(jnp.bfloat16)
```

```python
import jax
import jax.numpy as jnp
from jax import lax
from jax.experimental import pallas as pl
from jax.experimental.pallas import tpu as pltpu
from jax.sharding import PartitionSpec as P

MESH = pl.DeviceIdType.MESH
BF16 = jnp.bfloat16
F32 = jnp.float32
RY, RX, RZ = 8, 4, 4
ROWS, HALF, QUARTER, LANES = 448, 224, 112, 128
STEPS = ((0,), (7, 1), (6, 2), (5, 3), (4,))
NEAR_Z = (0, 1, 7, 2, 6, 3, 5, 4)
NEAR_ZH = (0, 1, 3, 2)
FAR_FIRST = ((0, 0), (1, 2), (0, 1), (1, 3), (0, 2), (1, 0), (0, 3), (1, 1))


def rem(a, b):
    return lax.rem(a, jnp.int32(b))


def div(a, b):
    return lax.div(a, jnp.int32(b))


def kernel(
    a_ref, g_ref, b_ref, out_ref,
    a_all, g_all, b_own, b_turned, b_all, f_part, c_out, c_in, z_out, z_in, h_all, part, relayed, x_in, x_sum, z_part, z_sum,
    loc, g_s, g_r, h_s, h_r, bz_s, bz_r, bm_s, bm_r, bp_s, bp_r, a_s, a_r, c_s, c_r, z_s, z_r,
    x_s, rel_r, x_r, zz_s, zz_r, last_s, last_r,
):
    row, col = lax.axis_index("row"), lax.axis_index("col")
    core = rem(row, 2)
    y = rem(div(row, 2), RY)
    zl = div(row, 2 * RY)
    x, zh = div(col, RZ), rem(col, RZ)
    own = zl * 2 + core

    def device(zl_=zl, y_=y, core_=core, x_=x, zh_=zh):
        return ((zl_ * RY + y_) * 2 + core_, x_ * RZ + zh_)

    y_to = (device(y_=rem(y + 1, RY)), device(y_=rem(y + RY - 1, RY)))
    x_up, x_down = device(x_=rem(x + 1, RX)), device(x_=rem(x + RX - 1, RX))
    core_other, zl_other = device(core_=1 - core), device(zl_=1 - zl)
    x_pair, x_mirror = device(x_=x + 1 - 2 * rem(x, 2)), device(x_=RX - 1 - x)

    def remote(src, dst, send, recv, to):
        return pltpu.make_async_remote_copy(
            src_ref=src, dst_ref=dst, send_sem=send, recv_sem=recv, device_id=to, device_id_type=MESH
        )

    def send(src, dst, s, r, to):
        remote(src, dst, s, r, to).start()

    def sent(src, s):
        remote(src, src, s, s, core_other).wait_send()

    def arrived(dst, r):
        remote(dst, dst, r, r, core_other).wait_recv()

    loads = [
        pltpu.make_async_copy(g_ref, g_all.at[y], loc.at[0]),
        pltpu.make_async_copy(b_ref.at[:, pl.ds(0, LANES)], b_own.at[0], loc.at[1]),
        pltpu.make_async_copy(b_ref.at[:, pl.ds(LANES, LANES)], b_own.at[1], loc.at[2]),
        pltpu.make_async_copy(a_ref, a_all.at[own], loc.at[3]),
    ]
    for load in loads:
        load.start()
    barrier = pltpu.get_barrier_semaphore()
    place = (zh * 2 + zl) * 2 + core
    for step in range(1, 16):
        there = rem(place + step, 16)
        pl.semaphore_signal(
            barrier,
            inc=1,
            device_id=device(zl_=rem(div(there, 2), 2), core_=rem(there, 2), zh_=div(there, 4)),
            device_id_type=MESH,
        )
    for to in (*y_to, x_up, x_down):
        pl.semaphore_signal(barrier, inc=1, device_id=to, device_id_type=MESH)
    from_zl = 1 - rem(div(x, 2) + rem(zh, 2), 2)
    from_x = rem(x + 2 * core + 1 - zl, RX)

    def from_here(half, q):
        return (x == from_x) & (zl == from_zl) & (core == half) & (zh == q)

    for half in range(2):
        for q in range(RZ):

            @pl.when(jnp.logical_not(from_here(half, q)))
            def _():
                pl.semaphore_signal(
                    barrier,
                    inc=1,
                    device_id=device(zl_=from_zl, core_=jnp.int32(half), x_=from_x, zh_=jnp.int32(q)),
                    device_id_type=MESH,
                )

    for load in loads:
        load.wait()
    for h in range(2):
        b_turned[h] = b_own[h].astype(F32).T.astype(BF16)
    pl.semaphore_wait(barrier, 27 - jnp.where((x == from_x) & (zl == from_zl), 1, 0))

    def ring_part(buf, owner, i):
        return buf.at[owner, pl.ds(i * HALF, HALF)]

    def ring_send(buf, s, r, way, hop, i):
        owner = rem(y + (RY - hop if way == 0 else hop), RY)
        send(ring_part(buf, owner, i), ring_part(buf, owner, i), s.at[way, hop, i], r.at[way, hop, i], y_to[way])

    def ring_wait(buf, r, way, hop, i):
        owner = rem(y + (RY - hop - 1 if way == 0 else hop + 1), RY)
        arrived(ring_part(buf, owner, i), r.at[way, hop, i])

    def ring_hop(buf, s, r, hop):
        for way, i in FAR_FIRST:
            ring_wait(buf, r, way, hop - 1, i)
            if hop < 3 or i // 2 == way:
                ring_send(buf, s, r, way, hop, i)

    def ring_end(buf, r):
        for way, i in FAR_FIRST:
            if i // 2 == way:
                ring_wait(buf, r, way, 3, i)

    def ring_sent(buf, s):
        for way, i in FAR_FIRST:
            for hop in range(4):
                if hop < 3 or i // 2 == way:
                    sent(ring_part(buf, 0, i), s.at[way, hop, i])

    for way, i in FAR_FIRST:
        ring_send(g_all, g_s, g_r, way, 0, i)

    b_here = rem(x, 2) * 4
    b_zl = div(x, 2)

    b_source = zl == b_zl
    b_first = rem(rem(x, 2) + rem(b_zl + zl, 2), 2) * 4

    for e in NEAR_ZH:
        to_zh = rem(zh + e, RZ)
        for h in range(2):

            def away():
                send(
                    b_turned.at[h], b_all.at[b_here + zh, own], bz_s.at[h, e], bz_r.at[own, zh],
                    device(zl_=b_zl, core_=jnp.int32(h), zh_=to_zh),
                )

            if e == 0:

                @pl.when(b_source & (core == h))
                def _():
                    b_all[b_here + zh, own] = b_turned[h]

                pl.when(jnp.logical_not(b_source & (core == h)))(away)
            else:
                away()

    def chunk(half, i):
        there = rem(2 * zh + zl + NEAR_Z[i], 2 * RZ)
        return b_all.at[half + div(there, 2), pl.ds(2 * rem(there, 2), 2)]

    def b_start(first, last):
        @pl.when(b_source)
        def _():
            for i in range(first, last):
                there = rem(2 * zh + zl + NEAR_Z[i], 2 * RZ)
                for c in range(2) if i > 0 else (1 - core,):
                    s = 2 * rem(there, 2) + c
                    arrived(b_all.at[b_here + div(there, 2), s], bz_r.at[s, div(there, 2)])
                block = chunk(b_here, i)
                send(block, block, bm_s.at[i], bm_r.at[i], x_mirror)
                send(block, block, bp_s.at[i], bp_r.at[i], x_pair)

    def b_forward(first, last):
        @pl.when(jnp.logical_not(b_source))
        def _():
            for i in range(first, last):
                block = chunk(b_first, i)
                arrived(block, bm_r.at[i])
                send(block, block, bp_s.at[i], bp_r.at[i], x_pair)

    b_start(0, 3)
    ring_hop(g_all, g_s, g_r, 1)
    b_start(3, 8)
    send(a_all.at[own], a_all.at[own], a_s.at[0], a_r.at[0], zl_other)
    send(a_all.at[own], a_all.at[own], a_s.at[1], a_r.at[1], core_other)
    b_forward(0, 3)
    ring_hop(g_all, g_s, g_r, 2)
    b_forward(3, 8)
    ring_hop(g_all, g_s, g_r, 3)
    ring_end(g_all, g_r)
    for i in range(2 * RZ):
        arrived(chunk(4 - b_first, i), bp_r.at[i])

    mine = rem(zl + y, 2)
    right = jnp.concatenate([b_all[:, t].reshape(RY * LANES, LANES) for t in range(4)], axis=1)
    for m in range(5):
        if m < 4:
            rows = pl.ds(m * HALF, HALF)
            left = jnp.concatenate([g_all[j, rows] for j in range(RY)], axis=1)
            share = jnp.dot(left, right, preferred_element_type=F32)
            for t in range(4):
                f_part[m, t] = share[:, t * LANES : (t + 1) * LANES]
            for t in range(2):
                c_out[m, t] = f_part[m, 2 * t + 1 - core].astype(BF16)
            send(c_out.at[m], c_in.at[m], c_s.at[m], c_r.at[m], core_other)
        if m >= 1:
            arrived(c_in.at[m - 1], c_r.at[m - 1])
            z_out[m - 1] = (
                f_part[m - 1, 2 * (1 - mine) + core] + c_in[m - 1, 1 - mine].astype(F32)
            ).astype(BF16)
            send(z_out.at[m - 1], z_in.at[m - 1], z_s.at[m - 1], z_r.at[m - 1], zl_other)
    a_next = a_all.at[2 * (1 - zl) + core]
    arrived(a_next, a_r.at[0])
    send(a_next, a_next, a_s.at[2], a_r.at[2], core_other)
    for m in range(4):
        arrived(z_in.at[m], z_r.at[m])
        h_all[y, pl.ds(m * HALF, HALF)] = (
            f_part[m, 2 * mine + core] + c_in[m, mine].astype(F32) + z_in[m].astype(F32)
        ).astype(BF16)
        for way in range(2):
            ring_send(h_all, h_s, h_r, way, 0, m)
    arrived(a_all.at[2 * zl + 1 - core], a_r.at[1])
    arrived(a_all.at[2 * (1 - zl) + 1 - core], a_r.at[2])

    def owner_x(o, plane):
        yy = rem(y + o, RY)
        return 2 * rem(plane + yy, 2) + div(yy, 4)

    def rows_at(o, at_x):
        away = rem(at_x + RX - owner_x(o, zl), RX)
        return 2 * (1 - rem(away, 2)) + div(away, 2)

    def multiply(step, s):
        offsets = STEPS[step]
        right = jnp.concatenate([h_all[rem(y + o, RY)] for o in offsets], axis=1)
        product = jnp.dot(a_all[s], right, preferred_element_type=F32).astype(BF16)
        for i, o in enumerate(offsets):
            to_x = rem(owner_x(o, zl) + 2 * rem(s, 2) + 1 - div(s, 2), RX)
            for half in range(2):
                part[step, to_x, half, i] = product[half * HALF : (half + 1) * HALF, i * LANES : (i + 1) * LANES]

    def count(step):
        return pl.ds(0, len(STEPS[step]))

    s_up, s_down, s_far = rem(x + 1, RX), rem(x + RX - 1, RX), rem(x + 2, RX)

    def x_send(step):
        n = count(step)
        if len(STEPS[step]) == 1:
            o = STEPS[step][0]
            multiply(step, rows_at(o, s_far))
        else:
            lax.fori_loop(0, 4, lambda i, carry: (multiply(step, i), carry)[1], 0)
        send(part.at[step, s_far, 0, n], relayed.at[step, 0, n], x_s.at[step, 0], rel_r.at[step, 0], x_down)
        send(part.at[step, s_far, 1, n], relayed.at[step, 1, n], x_s.at[step, 1], rel_r.at[step, 1], x_up)
        if len(STEPS[step]) == 1:
            lax.fori_loop(3, 6, lambda i, carry: (multiply(step, rows_at(o, rem(x + i, RX))), carry)[1], 0)
        send(part.at[step, s_down, 1, n], x_in.at[step, 0, 1, n], x_s.at[step, 2], x_r.at[step, 0, 1], x_down)
        send(part.at[step, s_up, 0, n], x_in.at[step, 1, 0, n], x_s.at[step, 3], x_r.at[step, 1, 0], x_up)

    def x_relay(step):
        n = count(step)
        for half, s, to in ((0, s_down, x_down), (1, s_up, x_up)):
            arrived(relayed.at[step, half, n], rel_r.at[step, half])
            for i in range(len(STEPS[step])):
                part[step, s, half, i] = (
                    part[step, s, half, i].astype(F32) + relayed[step, half, i].astype(F32)
                ).astype(BF16)
            send(
                part.at[step, s, half, n], x_in.at[step, half, half, n], x_s.at[step, 4 + half],
                x_r.at[step, half, half], to,
            )

    def z_send(step):
        n = count(step)
        for half in range(2):
            for side in range(2):
                arrived(x_in.at[step, side, half, n], x_r.at[step, side, half])
            for i in range(len(STEPS[step])):
                total = (
                    part[step, x, half, i].astype(F32)
                    + x_in[step, 0, half, i].astype(F32)
                    + x_in[step, 1, half, i].astype(F32)
                ).astype(BF16)
                for q in range(2):
                    x_sum[step, 2 * half + q, i] = total[q * QUARTER : (q + 1) * QUARTER]
            for q in range(2 * half, 2 * half + 2):
                send(
                    x_sum.at[step, q, n], z_part.at[step, zh, n], zz_s.at[step, q], zz_r.at[step, zh],
                    device(zl_=1 - zl, zh_=jnp.int32(q)),
                )

    def owner(o):
        to_x = owner_x(o, 1 - zl)
        away = rem(x + RX - to_x, RX)
        return 1 - rem(away, 2), div(away, 2), to_x, rem(rem(y + o, RY), 4)

    def owned_here(o):
        to_zl, to_core, to_x, to_zh = owner(o)
        return (zl == to_zl) & (core == to_core) & (to_x == x) & (to_zh == zh)

    def piece(half, q):
        return out_ref.at[pl.ds(q * QUARTER, QUARTER), pl.ds(pl.multiple_of(half * LANES, LANES), LANES)]

    def last_send(step):
        n = count(step)
        for s in range(RZ):
            arrived(z_part.at[step, s, n], zz_r.at[step, s])
        for i, o in enumerate(STEPS[step]):
            total = z_part[step, 0, i].astype(F32)
            for s in range(1, RZ):
                total = total + z_part[step, s, i].astype(F32)
            z_sum[o] = total.astype(BF16)
            to_zl, to_core, to_x, to_zh = owner(o)

            @pl.when(owned_here(o))
            def _():
                pltpu.make_async_copy(z_sum.at[o], piece(core, zh), last_s.at[o]).start()

            @pl.when(jnp.logical_not(owned_here(o)))
            def _():
                send(
                    z_sum.at[o], piece(core, zh), last_s.at[o], last_r.at[core, zh],
                    device(zl_=to_zl, core_=to_core, x_=to_x, zh_=to_zh),
                )

    for step in range(len(STEPS) + 2):
        if 1 <= step <= 3:
            ring_hop(h_all, h_s, h_r, step)
        if step == 4:
            ring_end(h_all, h_r)
        for stage, back in ((x_send, 0), (x_relay, 0), (z_send, 1), (last_send, 2)):
            if 0 <= step - back < len(STEPS):
                stage(step - back)

    ring_sent(g_all, g_s)
    ring_sent(h_all, h_s)
    for e in NEAR_ZH:
        for h in range(2):

            def left_here():
                sent(b_turned.at[h], bz_s.at[h, e])

            if e == 0:
                pl.when(jnp.logical_not(b_source & (core == h)))(left_here)
            else:
                left_here()

    for i in range(2 * RZ):
        sent(chunk(0, i), bp_s.at[i])

    @pl.when(b_source)
    def _():
        for i in range(2 * RZ):
            sent(chunk(0, i), bm_s.at[i])

    for i in range(3):
        sent(a_all.at[0], a_s.at[i])
    for m in range(4):
        sent(c_out.at[m], c_s.at[m])
        sent(z_out.at[m], z_s.at[m])
    for step in range(len(STEPS)):
        n = count(step)
        for i in range(6):
            sent(part.at[step, 0, 0, n], x_s.at[step, i])
        for q in range(RZ):
            sent(x_sum.at[step, q, n], zz_s.at[step, q])
    for o in range(RY):

        @pl.when(owned_here(o))
        def _():
            pltpu.make_async_copy(z_sum.at[o], piece(core, zh), last_s.at[o]).wait()

        @pl.when(jnp.logical_not(owned_here(o)))
        def _():
            sent(z_sum.at[o], last_s.at[o])

    for half in range(2):
        for q in range(RZ):

            @pl.when(jnp.logical_not(from_here(half, q)))
            def _():
                arrived(piece(jnp.int32(half), jnp.int32(q)), last_r.at[half, q])


def body(out_inverse, gradient, in_inverse):
    dma = pltpu.SemaphoreType.DMA
    vmem = pltpu.VMEM
    return pl.pallas_call(
        kernel,
        out_shape=jax.ShapeDtypeStruct((ROWS, 2 * LANES), BF16),
        in_specs=[pl.BlockSpec(memory_space=pl.ANY)] * 3,
        out_specs=pl.BlockSpec(memory_space=pl.ANY),
        scratch_shapes=[
            vmem((4, ROWS, 2 * ROWS), BF16),
            vmem((RY, 2 * ROWS, LANES), BF16),
            vmem((2, LANES, LANES), BF16),
            vmem((2, LANES, LANES), BF16),
            vmem((RY, 4, LANES, LANES), BF16),
            vmem((4, 4, HALF, LANES), F32),
            vmem((4, 2, HALF, LANES), BF16),
            vmem((4, 2, HALF, LANES), BF16),
            vmem((4, HALF, LANES), BF16),
            vmem((4, HALF, LANES), BF16),
            vmem((RY, 2 * ROWS, LANES), BF16),
            vmem((5, 4, 2, 2, HALF, LANES), BF16),
            vmem((5, 2, 2, HALF, LANES), BF16),
            vmem((5, 2, 2, 2, HALF, LANES), BF16),
            vmem((5, RZ, 2, QUARTER, LANES), BF16),
            vmem((5, RZ, 2, QUARTER, LANES), BF16),
            vmem((RY, QUARTER, LANES), BF16),
            dma((4,)),
            dma((2, 4, 4)), dma((2, 4, 4)),
            dma((2, 4, 4)), dma((2, 4, 4)),
            dma((2, RZ)), dma((4, RZ)),
            dma((2 * RZ,)), dma((2 * RZ,)),
            dma((2 * RZ,)), dma((2 * RZ,)),
            dma((3,)), dma((3,)),
            dma((4,)), dma((4,)),
            dma((4,)), dma((4,)),
            dma((5, 6)), dma((5, 2)), dma((5, 2, 2)),
            dma((5, RZ)), dma((5, RZ)),
            dma((RY,)), dma((2, RZ)),
        ],
        compiler_params=pltpu.CompilerParams(
            collective_id=0, has_side_effects=True, vmem_limit_bytes=64 * 1024 * 1024
        ),
        cost_estimate=pl.CostEstimate(flops=4_300_000_000, bytes_accessed=2_000_000, transcendentals=0),
    )(out_inverse, gradient, in_inverse)


def solution(mesh):
    in_specs = (P("row", "col"), P("col", "row"), P("row", "col"))
    return jax.shard_map(body, mesh=mesh, in_specs=in_specs, out_specs=P("row", "col"), check_vma=False)
```

```python
import jax
import jax.numpy as jnp
from jax import lax
from jax.experimental import pallas as pl
from jax.experimental.pallas import tpu as pltpu
from jax.sharding import PartitionSpec as P

MESH = pl.DeviceIdType.MESH
BF16 = jnp.bfloat16
F32 = jnp.float32
RY, RX, RZ = 8, 4, 4
ROWS, HALF, QUARTER, LANES = 448, 224, 112, 128
STEPS = ((0,), (7, 1), (6, 2), (5, 3), (4,))
NEAR_Z = (0, 1, 7, 2, 6, 3, 5, 4)
NEAR_ZH = (0, 1, 3, 2)
FAR_FIRST = ((0, 0), (1, 2), (0, 1), (1, 3), (0, 2), (1, 0), (0, 3), (1, 1))


def rem(a, b):
    return lax.rem(a, jnp.int32(b))


def div(a, b):
    return lax.div(a, jnp.int32(b))


def kernel(
    a_ref, g_ref, b_ref, out_ref,
    a_all, g_all, b_own, b_turned, b_all, f_part, c_out, c_in, z_out, z_in, h_all, part, relayed, x_in, x_sum, z_part, z_sum,
    loc, g_s, g_r, h_s, h_r, bz_s, bz_r, bm_s, bm_r, bp_s, bp_r, a_s, a_r, c_s, c_r, z_s, z_r,
    x_s, rel_r, x_r, zz_s, zz_r, last_s, last_r,
):
    row, col = lax.axis_index("row"), lax.axis_index("col")
    core = rem(row, 2)
    y = rem(div(row, 2), RY)
    zl = div(row, 2 * RY)
    x, zh = div(col, RZ), rem(col, RZ)
    own = zl * 2 + core

    def device(zl_=zl, y_=y, core_=core, x_=x, zh_=zh):
        return ((zl_ * RY + y_) * 2 + core_, x_ * RZ + zh_)

    y_to = (device(y_=rem(y + 1, RY)), device(y_=rem(y + RY - 1, RY)))
    x_up, x_down = device(x_=rem(x + 1, RX)), device(x_=rem(x + RX - 1, RX))
    core_other, zl_other = device(core_=1 - core), device(zl_=1 - zl)
    x_pair, x_mirror = device(x_=x + 1 - 2 * rem(x, 2)), device(x_=RX - 1 - x)

    def remote(src, dst, send, recv, to):
        return pltpu.make_async_remote_copy(
            src_ref=src, dst_ref=dst, send_sem=send, recv_sem=recv, device_id=to, device_id_type=MESH
        )

    def send(src, dst, s, r, to):
        remote(src, dst, s, r, to).start()

    def sent(src, s):
        remote(src, src, s, s, core_other).wait_send()

    def arrived(dst, r):
        remote(dst, dst, r, r, core_other).wait_recv()

    loads = [
        pltpu.make_async_copy(g_ref, g_all.at[y], loc.at[0]),
        pltpu.make_async_copy(b_ref.at[:, pl.ds(0, LANES)], b_own.at[0], loc.at[1]),
        pltpu.make_async_copy(b_ref.at[:, pl.ds(LANES, LANES)], b_own.at[1], loc.at[2]),
        pltpu.make_async_copy(a_ref, a_all.at[own], loc.at[3]),
    ]
    for load in loads:
        load.start()
    barrier = pltpu.get_barrier_semaphore()
    place = (zh * 2 + zl) * 2 + core
    for step in range(1, 16):
        there = rem(place + step, 16)
        pl.semaphore_signal(
            barrier,
            inc=1,
            device_id=device(zl_=rem(div(there, 2), 2), core_=rem(there, 2), zh_=div(there, 4)),
            device_id_type=MESH,
        )
    for to in (*y_to, x_up, x_down):
        pl.semaphore_signal(barrier, inc=1, device_id=to, device_id_type=MESH)
    from_zl = 1 - rem(div(x, 2) + rem(zh, 2), 2)
    from_x = rem(x + 2 * core + 1 - zl, RX)

    def from_here(half, q):
        return (x == from_x) & (zl == from_zl) & (core == half) & (zh == q)

    for half in range(2):
        for q in range(RZ):

            @pl.when(jnp.logical_not(from_here(half, q)))
            def _():
                pl.semaphore_signal(
                    barrier,
                    inc=1,
                    device_id=device(zl_=from_zl, core_=jnp.int32(half), x_=from_x, zh_=jnp.int32(q)),
                    device_id_type=MESH,
                )

    for load in loads:
        load.wait()
    for h in range(2):
        b_turned[h] = b_own[h].astype(F32).T.astype(BF16)
    pl.semaphore_wait(barrier, 27 - jnp.where((x == from_x) & (zl == from_zl), 1, 0))

    def ring_part(buf, owner, i):
        return buf.at[owner, pl.ds(i * HALF, HALF)]

    def ring_send(buf, s, r, way, hop, i):
        owner = rem(y + (RY - hop if way == 0 else hop), RY)
        send(ring_part(buf, owner, i), ring_part(buf, owner, i), s.at[way, hop, i], r.at[way, hop, i], y_to[way])

    def ring_wait(buf, r, way, hop, i):
        owner = rem(y + (RY - hop - 1 if way == 0 else hop + 1), RY)
        arrived(ring_part(buf, owner, i), r.at[way, hop, i])

    def ring_hop(buf, s, r, hop):
        for way, i in FAR_FIRST:
            ring_wait(buf, r, way, hop - 1, i)
            if hop < 3 or i // 2 == way:
                ring_send(buf, s, r, way, hop, i)

    def ring_end(buf, r):
        for way, i in FAR_FIRST:
            if i // 2 == way:
                ring_wait(buf, r, way, 3, i)

    def ring_sent(buf, s, hop):
        for way, i in FAR_FIRST:
            if hop < 3 or i // 2 == way:
                sent(ring_part(buf, 0, i), s.at[way, hop, i])

    for way, i in FAR_FIRST:
        ring_send(g_all, g_s, g_r, way, 0, i)

    b_here = rem(x, 2) * 4
    b_zl = div(x, 2)

    b_source = zl == b_zl
    b_first = rem(rem(x, 2) + rem(b_zl + zl, 2), 2) * 4

    for e in NEAR_ZH:
        to_zh = rem(zh + e, RZ)
        for h in range(2):

            def away():
                send(
                    b_turned.at[h], b_all.at[b_here + zh, own], bz_s.at[h, e], bz_r.at[own, zh],
                    device(zl_=b_zl, core_=jnp.int32(h), zh_=to_zh),
                )

            if e == 0:

                @pl.when(b_source & (core == h))
                def _():
                    b_all[b_here + zh, own] = b_turned[h]

                pl.when(jnp.logical_not(b_source & (core == h)))(away)
            else:
                away()

    def chunk(half, i):
        there = rem(2 * zh + zl + NEAR_Z[i], 2 * RZ)
        return b_all.at[half + div(there, 2), pl.ds(2 * rem(there, 2), 2)]

    def b_start(first, last):
        @pl.when(b_source)
        def _():
            for i in range(first, last):
                there = rem(2 * zh + zl + NEAR_Z[i], 2 * RZ)
                for c in range(2) if i > 0 else (1 - core,):
                    s = 2 * rem(there, 2) + c
                    arrived(b_all.at[b_here + div(there, 2), s], bz_r.at[s, div(there, 2)])
                block = chunk(b_here, i)
                send(block, block, bm_s.at[i], bm_r.at[i], x_mirror)
                send(block, block, bp_s.at[i], bp_r.at[i], x_pair)

    def b_forward(first, last):
        @pl.when(jnp.logical_not(b_source))
        def _():
            for i in range(first, last):
                block = chunk(b_first, i)
                arrived(block, bm_r.at[i])
                send(block, block, bp_s.at[i], bp_r.at[i], x_pair)

    b_start(0, 3)
    ring_hop(g_all, g_s, g_r, 1)
    b_start(3, 8)
    send(a_all.at[own], a_all.at[own], a_s.at[0], a_r.at[0], zl_other)
    send(a_all.at[own], a_all.at[own], a_s.at[1], a_r.at[1], core_other)
    b_forward(0, 3)
    ring_hop(g_all, g_s, g_r, 2)
    b_forward(3, 8)
    ring_hop(g_all, g_s, g_r, 3)
    ring_end(g_all, g_r)
    for i in range(2 * RZ):
        arrived(chunk(4 - b_first, i), bp_r.at[i])

    mine = rem(zl + y, 2)
    right = jnp.concatenate([b_all[:, t].reshape(RY * LANES, LANES) for t in range(4)], axis=1)
    for m in range(5):
        if m < 4:
            rows = pl.ds(m * HALF, HALF)
            left = jnp.concatenate([g_all[j, rows] for j in range(RY)], axis=1)
            share = jnp.dot(left, right, preferred_element_type=F32)
            for t in range(4):
                f_part[m, t] = share[:, t * LANES : (t + 1) * LANES]
            for t in range(2):
                c_out[m, t] = f_part[m, 2 * t + 1 - core].astype(BF16)
            send(c_out.at[m], c_in.at[m], c_s.at[m], c_r.at[m], core_other)
        if m >= 1:
            arrived(c_in.at[m - 1], c_r.at[m - 1])
            z_out[m - 1] = (
                f_part[m - 1, 2 * (1 - mine) + core] + c_in[m - 1, 1 - mine].astype(F32)
            ).astype(BF16)
            send(z_out.at[m - 1], z_in.at[m - 1], z_s.at[m - 1], z_r.at[m - 1], zl_other)
    a_next = a_all.at[2 * (1 - zl) + core]
    arrived(a_next, a_r.at[0])
    send(a_next, a_next, a_s.at[2], a_r.at[2], core_other)
    for m in range(4):
        arrived(z_in.at[m], z_r.at[m])
        h_all[y, pl.ds(m * HALF, HALF)] = (
            f_part[m, 2 * mine + core] + c_in[m, mine].astype(F32) + z_in[m].astype(F32)
        ).astype(BF16)
        for way in range(2):
            ring_send(h_all, h_s, h_r, way, 0, m)
    arrived(a_all.at[2 * zl + 1 - core], a_r.at[1])
    arrived(a_all.at[2 * (1 - zl) + 1 - core], a_r.at[2])

    def owner_x(o, plane):
        yy = rem(y + o, RY)
        return 2 * rem(plane + yy, 2) + div(yy, 4)

    def rows_at(o, at_x):
        away = rem(at_x + RX - owner_x(o, zl), RX)
        return 2 * (1 - rem(away, 2)) + div(away, 2)

    def multiply(step, s):
        offsets = STEPS[step]
        right = jnp.concatenate([h_all[rem(y + o, RY)] for o in offsets], axis=1)
        product = jnp.dot(a_all[s], right, preferred_element_type=F32).astype(BF16)
        for i, o in enumerate(offsets):
            to_x = rem(owner_x(o, zl) + 2 * rem(s, 2) + 1 - div(s, 2), RX)
            for half in range(2):
                part[step, to_x, half, i] = product[half * HALF : (half + 1) * HALF, i * LANES : (i + 1) * LANES]

    def count(step):
        return pl.ds(0, len(STEPS[step]))

    s_up, s_down, s_far = rem(x + 1, RX), rem(x + RX - 1, RX), rem(x + 2, RX)

    def x_send(step):
        n = count(step)
        if len(STEPS[step]) == 1:
            o = STEPS[step][0]
            multiply(step, rows_at(o, s_far))
        else:
            lax.fori_loop(0, 4, lambda i, carry: (multiply(step, i), carry)[1], 0)
        send(part.at[step, s_far, 0, n], relayed.at[step, 0, n], x_s.at[step, 0], rel_r.at[step, 0], x_down)
        send(part.at[step, s_far, 1, n], relayed.at[step, 1, n], x_s.at[step, 1], rel_r.at[step, 1], x_up)
        if len(STEPS[step]) == 1:
            lax.fori_loop(3, 6, lambda i, carry: (multiply(step, rows_at(o, rem(x + i, RX))), carry)[1], 0)
        send(part.at[step, s_down, 1, n], x_in.at[step, 0, 1, n], x_s.at[step, 2], x_r.at[step, 0, 1], x_down)
        send(part.at[step, s_up, 0, n], x_in.at[step, 1, 0, n], x_s.at[step, 3], x_r.at[step, 1, 0], x_up)

    def x_relay(step):
        n = count(step)
        for half, s, to in ((0, s_down, x_down), (1, s_up, x_up)):
            arrived(relayed.at[step, half, n], rel_r.at[step, half])
            for i in range(len(STEPS[step])):
                part[step, s, half, i] = (
                    part[step, s, half, i].astype(F32) + relayed[step, half, i].astype(F32)
                ).astype(BF16)
            send(
                part.at[step, s, half, n], x_in.at[step, half, half, n], x_s.at[step, 4 + half],
                x_r.at[step, half, half], to,
            )

    def z_send(step):
        n = count(step)
        for half in range(2):
            for side in range(2):
                arrived(x_in.at[step, side, half, n], x_r.at[step, side, half])
            for i in range(len(STEPS[step])):
                total = (
                    part[step, x, half, i].astype(F32)
                    + x_in[step, 0, half, i].astype(F32)
                    + x_in[step, 1, half, i].astype(F32)
                ).astype(BF16)
                for q in range(2):
                    x_sum[step, 2 * half + q, i] = total[q * QUARTER : (q + 1) * QUARTER]
            for q in range(2 * half, 2 * half + 2):
                send(
                    x_sum.at[step, q, n], z_part.at[step, zh, n], zz_s.at[step, q], zz_r.at[step, zh],
                    device(zl_=1 - zl, zh_=jnp.int32(q)),
                )

    def owner(o):
        to_x = owner_x(o, 1 - zl)
        away = rem(x + RX - to_x, RX)
        return 1 - rem(away, 2), div(away, 2), to_x, rem(rem(y + o, RY), 4)

    def owned_here(o):
        to_zl, to_core, to_x, to_zh = owner(o)
        return (zl == to_zl) & (core == to_core) & (to_x == x) & (to_zh == zh)

    def piece(half, q):
        return out_ref.at[pl.ds(q * QUARTER, QUARTER), pl.ds(pl.multiple_of(half * LANES, LANES), LANES)]

    def last_send(step):
        n = count(step)
        for s in range(RZ):
            arrived(z_part.at[step, s, n], zz_r.at[step, s])
        for i, o in enumerate(STEPS[step]):
            total = z_part[step, 0, i].astype(F32)
            for s in range(1, RZ):
                total = total + z_part[step, s, i].astype(F32)
            z_sum[o] = total.astype(BF16)
            to_zl, to_core, to_x, to_zh = owner(o)

            @pl.when(owned_here(o))
            def _():
                pltpu.make_async_copy(z_sum.at[o], piece(core, zh), last_s.at[o]).start()

            @pl.when(jnp.logical_not(owned_here(o)))
            def _():
                send(
                    z_sum.at[o], piece(core, zh), last_s.at[o], last_r.at[core, zh],
                    device(zl_=to_zl, core_=to_core, x_=to_x, zh_=to_zh),
                )

    def g_sent():
        for hop in range(4):
            ring_sent(g_all, g_s, hop)

    def b_sent():
        for e in NEAR_ZH:
            for h in range(2):

                def left_here():
                    sent(b_turned.at[h], bz_s.at[h, e])

                if e == 0:
                    pl.when(jnp.logical_not(b_source & (core == h)))(left_here)
                else:
                    left_here()

        for i in range(2 * RZ):
            sent(chunk(0, i), bp_s.at[i])

        @pl.when(b_source)
        def _():
            for i in range(2 * RZ):
                sent(chunk(0, i), bm_s.at[i])

    def a_sent():
        for i in range(3):
            sent(a_all.at[0], a_s.at[i])
        for m in range(4):
            sent(c_out.at[m], c_s.at[m])
            sent(z_out.at[m], z_s.at[m])
        ring_sent(h_all, h_s, 0)

    def steps_sent(step):
        n = count(step)
        for i in range(6):
            sent(part.at[step, 0, 0, n], x_s.at[step, i])
        for q in range(RZ):
            sent(x_sum.at[step, q, n], zz_s.at[step, q])

    def all_sent(step):
        if step == 0:
            g_sent()
        elif step == 1:
            b_sent()
        elif step == 2:
            a_sent()
        else:
            ring_sent(h_all, h_s, step - 2)
            steps_sent(step - 3)

    for step in range(len(STEPS) + 2):
        if 1 <= step <= 3:
            ring_hop(h_all, h_s, h_r, step)
        if step == 4:
            ring_end(h_all, h_r)
        if step < len(STEPS):
            x_send(step)
            all_sent(step)
            x_relay(step)
        for stage, back in ((z_send, 1), (last_send, 2)):
            if 0 <= step - back < len(STEPS):
                stage(step - back)
        if step == 5:
            steps_sent(2)

    ring_sent(h_all, h_s, 3)
    steps_sent(3)
    steps_sent(4)
    for o in range(RY):

        @pl.when(owned_here(o))
        def _():
            pltpu.make_async_copy(z_sum.at[o], piece(core, zh), last_s.at[o]).wait()

        @pl.when(jnp.logical_not(owned_here(o)))
        def _():
            sent(z_sum.at[o], last_s.at[o])

    for half in range(2):
        for q in range(RZ):

            @pl.when(jnp.logical_not(from_here(half, q)))
            def _():
                arrived(piece(jnp.int32(half), jnp.int32(q)), last_r.at[half, q])


def body(out_inverse, gradient, in_inverse):
    dma = pltpu.SemaphoreType.DMA
    vmem = pltpu.VMEM
    return pl.pallas_call(
        kernel,
        out_shape=jax.ShapeDtypeStruct((ROWS, 2 * LANES), BF16),
        in_specs=[pl.BlockSpec(memory_space=pl.ANY)] * 3,
        out_specs=pl.BlockSpec(memory_space=pl.ANY),
        scratch_shapes=[
            vmem((4, ROWS, 2 * ROWS), BF16),
            vmem((RY, 2 * ROWS, LANES), BF16),
            vmem((2, LANES, LANES), BF16),
            vmem((2, LANES, LANES), BF16),
            vmem((RY, 4, LANES, LANES), BF16),
            vmem((4, 4, HALF, LANES), F32),
            vmem((4, 2, HALF, LANES), BF16),
            vmem((4, 2, HALF, LANES), BF16),
            vmem((4, HALF, LANES), BF16),
            vmem((4, HALF, LANES), BF16),
            vmem((RY, 2 * ROWS, LANES), BF16),
            vmem((5, 4, 2, 2, HALF, LANES), BF16),
            vmem((5, 2, 2, HALF, LANES), BF16),
            vmem((5, 2, 2, 2, HALF, LANES), BF16),
            vmem((5, RZ, 2, QUARTER, LANES), BF16),
            vmem((5, RZ, 2, QUARTER, LANES), BF16),
            vmem((RY, QUARTER, LANES), BF16),
            dma((4,)),
            dma((2, 4, 4)), dma((2, 4, 4)),
            dma((2, 4, 4)), dma((2, 4, 4)),
            dma((2, RZ)), dma((4, RZ)),
            dma((2 * RZ,)), dma((2 * RZ,)),
            dma((2 * RZ,)), dma((2 * RZ,)),
            dma((3,)), dma((3,)),
            dma((4,)), dma((4,)),
            dma((4,)), dma((4,)),
            dma((5, 6)), dma((5, 2)), dma((5, 2, 2)),
            dma((5, RZ)), dma((5, RZ)),
            dma((RY,)), dma((2, RZ)),
        ],
        compiler_params=pltpu.CompilerParams(
            collective_id=0, has_side_effects=True, vmem_limit_bytes=64 * 1024 * 1024
        ),
        cost_estimate=pl.CostEstimate(flops=4_300_000_000, bytes_accessed=2_000_000, transcendentals=0),
    )(out_inverse, gradient, in_inverse)


def solution(mesh):
    in_specs = (P("row", "col"), P("col", "row"), P("row", "col"))
    return jax.shard_map(body, mesh=mesh, in_specs=in_specs, out_specs=P("row", "col"), check_vma=False)
```

```python
import jax
import jax.numpy as jnp
from jax import lax
from jax.experimental import pallas as pl
from jax.experimental.pallas import tpu as pltpu
from jax.sharding import PartitionSpec as P

MESH = pl.DeviceIdType.MESH
BF16 = jnp.bfloat16
F32 = jnp.float32
RY, RX, RZ = 8, 4, 4
ROWS, HALF, QUARTER, LANES = 448, 224, 112, 128
STEPS = ((0,), (7, 1), (6, 2), (5, 3), (4,))
NEAR_Z = (0, 1, 7, 2, 6, 3, 5, 4)
NEAR_ZH = (0, 1, 3, 2)
FAR_FIRST = ((0, 0), (1, 2), (0, 1), (1, 3), (0, 2), (1, 0), (0, 3), (1, 1))


def rem(a, b):
    return lax.rem(a, jnp.int32(b))


def div(a, b):
    return lax.div(a, jnp.int32(b))


def kernel(
    a_ref, g_ref, b_ref, out_ref,
    a_all, g_all, b_own, b_turned, b_all, f_part, c_out, c_in, z_out, z_in, h_all, part, relayed, x_in, x_sum, z_part, z_sum,
    loc, g_s, g_r, h_s, h_r, bz_s, bz_r, bm_s, bm_r, bp_s, bp_r, a_s, a_r, c_s, c_r, z_s, z_r,
    x_s, rel_r, x_r, zz_s, zz_r, last_s, last_r,
):
    row, col = lax.axis_index("row"), lax.axis_index("col")
    core = rem(row, 2)
    y = rem(div(row, 2), RY)
    zl = div(row, 2 * RY)
    x, zh = div(col, RZ), rem(col, RZ)
    own = zl * 2 + core

    def device(zl_=zl, y_=y, core_=core, x_=x, zh_=zh):
        return ((zl_ * RY + y_) * 2 + core_, x_ * RZ + zh_)

    y_to = (device(y_=rem(y + 1, RY)), device(y_=rem(y + RY - 1, RY)))
    x_up, x_down = device(x_=rem(x + 1, RX)), device(x_=rem(x + RX - 1, RX))
    core_other, zl_other = device(core_=1 - core), device(zl_=1 - zl)
    x_pair, x_mirror = device(x_=x + 1 - 2 * rem(x, 2)), device(x_=RX - 1 - x)

    def remote(src, dst, send, recv, to):
        return pltpu.make_async_remote_copy(
            src_ref=src, dst_ref=dst, send_sem=send, recv_sem=recv, device_id=to, device_id_type=MESH
        )

    def send(src, dst, s, r, to):
        remote(src, dst, s, r, to).start()

    def sent(src, s):
        remote(src, src, s, s, core_other).wait_send()

    def arrived(dst, r):
        remote(dst, dst, r, r, core_other).wait_recv()

    loads = [
        pltpu.make_async_copy(g_ref, g_all.at[y], loc.at[0]),
        pltpu.make_async_copy(b_ref.at[:, pl.ds(0, LANES)], b_own.at[0], loc.at[1]),
        pltpu.make_async_copy(b_ref.at[:, pl.ds(LANES, LANES)], b_own.at[1], loc.at[2]),
        pltpu.make_async_copy(a_ref, a_all.at[own], loc.at[3]),
    ]
    for load in loads:
        load.start()
    barrier = pltpu.get_barrier_semaphore()
    place = (zh * 2 + zl) * 2 + core
    for step in range(1, 16):
        there = rem(place + step, 16)
        pl.semaphore_signal(
            barrier,
            inc=1,
            device_id=device(zl_=rem(div(there, 2), 2), core_=rem(there, 2), zh_=div(there, 4)),
            device_id_type=MESH,
        )
    for to in (*y_to, x_up, x_down):
        pl.semaphore_signal(barrier, inc=1, device_id=to, device_id_type=MESH)
    from_zl = 1 - rem(div(x, 2) + rem(zh, 2), 2)
    from_x = rem(x + 2 * core + 1 - zl, RX)

    def from_here(half, q):
        return (x == from_x) & (zl == from_zl) & (core == half) & (zh == q)

    for half in range(2):
        for q in range(RZ):

            @pl.when(jnp.logical_not(from_here(half, q)))
            def _():
                pl.semaphore_signal(
                    barrier,
                    inc=1,
                    device_id=device(zl_=from_zl, core_=jnp.int32(half), x_=from_x, zh_=jnp.int32(q)),
                    device_id_type=MESH,
                )

    for load in loads:
        load.wait()
    for h in range(2):
        b_turned[h] = b_own[h].astype(F32).T.astype(BF16)
    pl.semaphore_wait(barrier, 27 - jnp.where((x == from_x) & (zl == from_zl), 1, 0))

    def ring_part(buf, owner, i):
        return buf.at[owner, pl.ds(i * HALF, HALF)]

    def ring_send(buf, s, r, way, hop, i):
        owner = rem(y + (RY - hop if way == 0 else hop), RY)
        send(ring_part(buf, owner, i), ring_part(buf, owner, i), s.at[way, hop, i], r.at[way, hop, i], y_to[way])

    def ring_wait(buf, r, way, hop, i):
        owner = rem(y + (RY - hop - 1 if way == 0 else hop + 1), RY)
        arrived(ring_part(buf, owner, i), r.at[way, hop, i])

    def ring_hop(buf, s, r, hop):
        for way, i in FAR_FIRST:
            ring_wait(buf, r, way, hop - 1, i)
            if hop < 3 or i // 2 == way:
                ring_send(buf, s, r, way, hop, i)

    def ring_end(buf, r):
        for way, i in FAR_FIRST:
            if i // 2 == way:
                ring_wait(buf, r, way, 3, i)

    def ring_sent(buf, s, hop):
        for way, i in FAR_FIRST:
            if hop < 3 or i // 2 == way:
                sent(ring_part(buf, 0, i), s.at[way, hop, i])

    for way, i in FAR_FIRST:
        ring_send(g_all, g_s, g_r, way, 0, i)

    b_here = rem(x, 2) * 4
    b_zl = div(x, 2)

    b_source = zl == b_zl
    b_first = rem(rem(x, 2) + rem(b_zl + zl, 2), 2) * 4

    for e in NEAR_ZH:
        to_zh = rem(zh + e, RZ)
        for h in range(2):

            def away():
                send(
                    b_turned.at[h], b_all.at[b_here + zh, own], bz_s.at[h, e], bz_r.at[own, zh],
                    device(zl_=b_zl, core_=jnp.int32(h), zh_=to_zh),
                )

            if e == 0:

                @pl.when(b_source & (core == h))
                def _():
                    b_all[b_here + zh, own] = b_turned[h]

                pl.when(jnp.logical_not(b_source & (core == h)))(away)
            else:
                away()

    def chunk(half, i):
        there = rem(2 * zh + zl + NEAR_Z[i], 2 * RZ)
        return b_all.at[half + div(there, 2), pl.ds(2 * rem(there, 2), 2)]

    def b_start(first, last):
        @pl.when(b_source)
        def _():
            for i in range(first, last):
                there = rem(2 * zh + zl + NEAR_Z[i], 2 * RZ)
                for c in range(2) if i > 0 else (1 - core,):
                    s = 2 * rem(there, 2) + c
                    arrived(b_all.at[b_here + div(there, 2), s], bz_r.at[s, div(there, 2)])
                block = chunk(b_here, i)
                send(block, block, bm_s.at[i], bm_r.at[i], x_mirror)
                send(block, block, bp_s.at[i], bp_r.at[i], x_pair)

    def b_forward(first, last):
        @pl.when(jnp.logical_not(b_source))
        def _():
            for i in range(first, last):
                block = chunk(b_first, i)
                arrived(block, bm_r.at[i])
                send(block, block, bp_s.at[i], bp_r.at[i], x_pair)

    b_start(0, 3)
    ring_hop(g_all, g_s, g_r, 1)
    b_start(3, 8)
    send(a_all.at[own], a_all.at[own], a_s.at[0], a_r.at[0], zl_other)
    send(a_all.at[own], a_all.at[own], a_s.at[1], a_r.at[1], core_other)
    b_forward(0, 3)
    ring_hop(g_all, g_s, g_r, 2)
    b_forward(3, 8)
    ring_hop(g_all, g_s, g_r, 3)
    ring_end(g_all, g_r)
    for i in range(2 * RZ):
        arrived(chunk(4 - b_first, i), bp_r.at[i])

    mine = rem(zl + y, 2)
    right = jnp.concatenate([b_all[:, t].reshape(RY * LANES, LANES) for t in range(4)], axis=1)
    for m in range(5):
        if m < 4:
            rows = pl.ds(m * HALF, HALF)
            left = jnp.concatenate([g_all[j, rows] for j in range(RY)], axis=1)
            share = jnp.dot(left, right, preferred_element_type=F32)
            for t in range(4):
                f_part[m, t] = share[:, t * LANES : (t + 1) * LANES]
            for t in range(2):
                c_out[m, t] = f_part[m, 2 * t + 1 - core].astype(BF16)
            send(c_out.at[m], c_in.at[m], c_s.at[m], c_r.at[m], core_other)
        if m >= 1:
            arrived(c_in.at[m - 1], c_r.at[m - 1])
            z_out[m - 1] = (
                f_part[m - 1, 2 * (1 - mine) + core] + c_in[m - 1, 1 - mine].astype(F32)
            ).astype(BF16)
            send(z_out.at[m - 1], z_in.at[m - 1], z_s.at[m - 1], z_r.at[m - 1], zl_other)
    a_next = a_all.at[2 * (1 - zl) + core]
    arrived(a_next, a_r.at[0])
    send(a_next, a_next, a_s.at[2], a_r.at[2], core_other)
    for m in range(4):
        arrived(z_in.at[m], z_r.at[m])
        h_all[y, pl.ds(m * HALF, HALF)] = (
            f_part[m, 2 * mine + core] + c_in[m, mine].astype(F32) + z_in[m].astype(F32)
        ).astype(BF16)
        for way in range(2):
            ring_send(h_all, h_s, h_r, way, 0, m)
    arrived(a_all.at[2 * zl + 1 - core], a_r.at[1])
    arrived(a_all.at[2 * (1 - zl) + 1 - core], a_r.at[2])

    def owner_x(o, plane):
        yy = rem(y + o, RY)
        return 2 * rem(plane + yy, 2) + div(yy, 4)

    def rows_at(o, at_x):
        away = rem(at_x + RX - owner_x(o, zl), RX)
        return 2 * (1 - rem(away, 2)) + div(away, 2)

    def multiply(step, s):
        offsets = STEPS[step]
        right = jnp.concatenate([h_all[rem(y + o, RY)] for o in offsets], axis=1)
        product = jnp.dot(a_all[s], right, preferred_element_type=F32).astype(BF16)
        for i, o in enumerate(offsets):
            to_x = rem(owner_x(o, zl) + 2 * rem(s, 2) + 1 - div(s, 2), RX)
            for half in range(2):
                part[step, to_x, half, i] = product[half * HALF : (half + 1) * HALF, i * LANES : (i + 1) * LANES]

    def count(step):
        return pl.ds(0, len(STEPS[step]))

    s_up, s_down, s_far = rem(x + 1, RX), rem(x + RX - 1, RX), rem(x + 2, RX)

    def x_send(step):
        n = count(step)
        if len(STEPS[step]) == 1:
            o = STEPS[step][0]
            multiply(step, rows_at(o, s_far))
        else:
            lax.fori_loop(0, 4, lambda i, carry: (multiply(step, i), carry)[1], 0)
        send(part.at[step, s_far, 0, n], relayed.at[step, 0, n], x_s.at[step, 0], rel_r.at[step, 0], x_down)
        send(part.at[step, s_far, 1, n], relayed.at[step, 1, n], x_s.at[step, 1], rel_r.at[step, 1], x_up)
        if len(STEPS[step]) == 1:
            lax.fori_loop(3, 6, lambda i, carry: (multiply(step, rows_at(o, rem(x + i, RX))), carry)[1], 0)
        send(part.at[step, s_down, 1, n], x_in.at[step, 0, 1, n], x_s.at[step, 2], x_r.at[step, 0, 1], x_down)
        send(part.at[step, s_up, 0, n], x_in.at[step, 1, 0, n], x_s.at[step, 3], x_r.at[step, 1, 0], x_up)

    def x_relay(step):
        n = count(step)
        for half, s, to in ((0, s_down, x_down), (1, s_up, x_up)):
            arrived(relayed.at[step, half, n], rel_r.at[step, half])
            for i in range(len(STEPS[step])):
                part[step, s, half, i] = (
                    part[step, s, half, i].astype(F32) + relayed[step, half, i].astype(F32)
                ).astype(BF16)
            send(
                part.at[step, s, half, n], x_in.at[step, half, half, n], x_s.at[step, 4 + half],
                x_r.at[step, half, half], to,
            )

    def z_send(step):
        n = count(step)
        for half in range(2):
            for side in range(2):
                arrived(x_in.at[step, side, half, n], x_r.at[step, side, half])
            for i in range(len(STEPS[step])):
                total = (
                    part[step, x, half, i].astype(F32)
                    + x_in[step, 0, half, i].astype(F32)
                    + x_in[step, 1, half, i].astype(F32)
                ).astype(BF16)
                for q in range(2):
                    x_sum[step, 2 * half + q, i] = total[q * QUARTER : (q + 1) * QUARTER]
            for q in range(2 * half, 2 * half + 2):
                send(
                    x_sum.at[step, q, n], z_part.at[step, zh, n], zz_s.at[step, q], zz_r.at[step, zh],
                    device(zl_=1 - zl, zh_=jnp.int32(q)),
                )

    def owner(o):
        to_x = owner_x(o, 1 - zl)
        away = rem(x + RX - to_x, RX)
        return 1 - rem(away, 2), div(away, 2), to_x, rem(rem(y + o, RY), 4)

    def owned_here(o):
        to_zl, to_core, to_x, to_zh = owner(o)
        return (zl == to_zl) & (core == to_core) & (to_x == x) & (to_zh == zh)

    def piece(half, q):
        return out_ref.at[pl.ds(q * QUARTER, QUARTER), pl.ds(pl.multiple_of(half * LANES, LANES), LANES)]

    def last_send(step):
        n = count(step)
        for s in range(RZ):
            arrived(z_part.at[step, s, n], zz_r.at[step, s])
        for i, o in enumerate(STEPS[step]):
            total = z_part[step, 0, i].astype(F32)
            for s in range(1, RZ):
                total = total + z_part[step, s, i].astype(F32)
            z_sum[o] = total.astype(BF16)
            to_zl, to_core, to_x, to_zh = owner(o)

            @pl.when(owned_here(o))
            def _():
                pltpu.make_async_copy(z_sum.at[o], piece(core, zh), last_s.at[o]).start()

            @pl.when(jnp.logical_not(owned_here(o)))
            def _():
                send(
                    z_sum.at[o], piece(core, zh), last_s.at[o], last_r.at[core, zh],
                    device(zl_=to_zl, core_=to_core, x_=to_x, zh_=to_zh),
                )

    def g_sent():
        for hop in range(4):
            ring_sent(g_all, g_s, hop)

    def b_sent():
        for e in NEAR_ZH:
            for h in range(2):

                def left_here():
                    sent(b_turned.at[h], bz_s.at[h, e])

                if e == 0:
                    pl.when(jnp.logical_not(b_source & (core == h)))(left_here)
                else:
                    left_here()

        for i in range(2 * RZ):
            sent(chunk(0, i), bp_s.at[i])

        @pl.when(b_source)
        def _():
            for i in range(2 * RZ):
                sent(chunk(0, i), bm_s.at[i])

    def a_sent():
        for i in range(3):
            sent(a_all.at[0], a_s.at[i])
        for m in range(4):
            sent(c_out.at[m], c_s.at[m])
            sent(z_out.at[m], z_s.at[m])
        ring_sent(h_all, h_s, 0)

    def steps_sent(step):
        n = count(step)
        for i in range(6):
            sent(part.at[step, 0, 0, n], x_s.at[step, i])
        for q in range(RZ):
            sent(x_sum.at[step, q, n], zz_s.at[step, q])

    def all_sent(step):
        if step == 0:
            g_sent()
        elif step == 1:
            b_sent()
        elif step == 2:
            a_sent()
        else:
            ring_sent(h_all, h_s, step - 2)
            steps_sent(step - 3)

    def x_stage(step):
        x_send(step)
        all_sent(step)
        x_relay(step)

    for step in range(3):
        if step >= 1:
            ring_hop(h_all, h_s, h_r, step)
        x_stage(step)
        if step >= 1:
            z_send(step - 1)
        if step >= 2:
            last_send(step - 2)
    ring_hop(h_all, h_s, h_r, 3)

    def finish(order):
        for step, before, last in zip(order, (2, order[0]), (1, 2)):
            if step == 4:
                ring_end(h_all, h_r)
            x_stage(step)
            z_send(before)
            last_send(last)
        z_send(order[1])
        last_send(order[0])
        last_send(order[1])

    @pl.when(rem(y, 4) == 0)
    def _():
        finish((4, 3))

    @pl.when(rem(y, 4) != 0)
    def _():
        finish((3, 4))

    ring_sent(h_all, h_s, 3)
    for step in range(2, 5):
        steps_sent(step)
    for o in range(RY):

        @pl.when(owned_here(o))
        def _():
            pltpu.make_async_copy(z_sum.at[o], piece(core, zh), last_s.at[o]).wait()

        @pl.when(jnp.logical_not(owned_here(o)))
        def _():
            sent(z_sum.at[o], last_s.at[o])

    for half in range(2):
        for q in range(RZ):

            @pl.when(jnp.logical_not(from_here(half, q)))
            def _():
                arrived(piece(jnp.int32(half), jnp.int32(q)), last_r.at[half, q])


def body(out_inverse, gradient, in_inverse):
    dma = pltpu.SemaphoreType.DMA
    vmem = pltpu.VMEM
    return pl.pallas_call(
        kernel,
        out_shape=jax.ShapeDtypeStruct((ROWS, 2 * LANES), BF16),
        in_specs=[pl.BlockSpec(memory_space=pl.ANY)] * 3,
        out_specs=pl.BlockSpec(memory_space=pl.ANY),
        scratch_shapes=[
            vmem((4, ROWS, 2 * ROWS), BF16),
            vmem((RY, 2 * ROWS, LANES), BF16),
            vmem((2, LANES, LANES), BF16),
            vmem((2, LANES, LANES), BF16),
            vmem((RY, 4, LANES, LANES), BF16),
            vmem((4, 4, HALF, LANES), F32),
            vmem((4, 2, HALF, LANES), BF16),
            vmem((4, 2, HALF, LANES), BF16),
            vmem((4, HALF, LANES), BF16),
            vmem((4, HALF, LANES), BF16),
            vmem((RY, 2 * ROWS, LANES), BF16),
            vmem((5, 4, 2, 2, HALF, LANES), BF16),
            vmem((5, 2, 2, HALF, LANES), BF16),
            vmem((5, 2, 2, 2, HALF, LANES), BF16),
            vmem((5, RZ, 2, QUARTER, LANES), BF16),
            vmem((5, RZ, 2, QUARTER, LANES), BF16),
            vmem((RY, QUARTER, LANES), BF16),
            dma((4,)),
            dma((2, 4, 4)), dma((2, 4, 4)),
            dma((2, 4, 4)), dma((2, 4, 4)),
            dma((2, RZ)), dma((4, RZ)),
            dma((2 * RZ,)), dma((2 * RZ,)),
            dma((2 * RZ,)), dma((2 * RZ,)),
            dma((3,)), dma((3,)),
            dma((4,)), dma((4,)),
            dma((4,)), dma((4,)),
            dma((5, 6)), dma((5, 2)), dma((5, 2, 2)),
            dma((5, RZ)), dma((5, RZ)),
            dma((RY,)), dma((2, RZ)),
        ],
        compiler_params=pltpu.CompilerParams(
            collective_id=0, has_side_effects=True, vmem_limit_bytes=64 * 1024 * 1024
        ),
        cost_estimate=pl.CostEstimate(flops=4_300_000_000, bytes_accessed=2_000_000, transcendentals=0),
    )(out_inverse, gradient, in_inverse)


def solution(mesh):
    in_specs = (P("row", "col"), P("col", "row"), P("row", "col"))
    return jax.shard_map(body, mesh=mesh, in_specs=in_specs, out_specs=P("row", "col"), check_vma=False)
```

```python
import jax
import jax.numpy as jnp
from jax import lax
from jax.experimental import pallas as pl
from jax.experimental.pallas import tpu as pltpu
from jax.sharding import PartitionSpec as P

MESH = pl.DeviceIdType.MESH
BF16 = jnp.bfloat16
F32 = jnp.float32
RY, RX, RZ = 8, 4, 4
ROWS, HALF, QUARTER, LANES = 448, 224, 112, 128
SLOTS = ((0,), (1, 2), (3, 4), (5, 6), (7,))
NEAR_Z = (0, 1, 7, 2, 6, 3, 5, 4)
NEAR_ZH = (0, 1, 3, 2)
FAR_FIRST = ((0, 0), (1, 2), (0, 1), (1, 3), (0, 2), (1, 0), (0, 3), (1, 1))
AS_MADE = ((0, 0), (1, 0), (0, 1), (1, 1), (0, 2), (1, 2), (0, 3), (1, 3))


def rem(a, b):
    return lax.rem(a, jnp.int32(b))


def div(a, b):
    return lax.div(a, jnp.int32(b))


def kernel(
    a_ref, g_ref, b_ref, out_ref,
    a_all, g_all, b_own, b_turned, b_all, f_part, c_out, c_in, z_out, z_in, h_all, part, relayed, x_in, x_sum, z_part, z_sum,
    loc, g_s, g_r, h_s, h_r, bz_s, bz_r, bm_s, bm_r, bp_s, bp_r, a_s, a_r, c_s, c_r, z_s, z_r,
    x_s, rel_r, x_r, zz_s, zz_r, last_s, last_r,
):
    row, col = lax.axis_index("row"), lax.axis_index("col")
    core = rem(row, 2)
    y = rem(div(row, 2), RY)
    zl = div(row, 2 * RY)
    x, zh = div(col, RZ), rem(col, RZ)
    own = zl * 2 + core

    def device(zl_=zl, y_=y, core_=core, x_=x, zh_=zh):
        return ((zl_ * RY + y_) * 2 + core_, x_ * RZ + zh_)

    y_to = (device(y_=rem(y + 1, RY)), device(y_=rem(y + RY - 1, RY)))
    x_up, x_down = device(x_=rem(x + 1, RX)), device(x_=rem(x + RX - 1, RX))
    core_other, zl_other = device(core_=1 - core), device(zl_=1 - zl)
    x_pair, x_mirror = device(x_=x + 1 - 2 * rem(x, 2)), device(x_=RX - 1 - x)

    def remote(src, dst, send, recv, to):
        return pltpu.make_async_remote_copy(
            src_ref=src, dst_ref=dst, send_sem=send, recv_sem=recv, device_id=to, device_id_type=MESH
        )

    def send(src, dst, s, r, to):
        remote(src, dst, s, r, to).start()

    def sent(src, s):
        remote(src, src, s, s, core_other).wait_send()

    def arrived(dst, r):
        remote(dst, dst, r, r, core_other).wait_recv()

    loads = [
        pltpu.make_async_copy(g_ref, g_all.at[y], loc.at[0]),
        pltpu.make_async_copy(b_ref.at[:, pl.ds(0, LANES)], b_own.at[0], loc.at[1]),
        pltpu.make_async_copy(b_ref.at[:, pl.ds(LANES, LANES)], b_own.at[1], loc.at[2]),
        pltpu.make_async_copy(a_ref, a_all.at[own], loc.at[3]),
    ]
    for load in loads:
        load.start()
    barrier = pltpu.get_barrier_semaphore()
    place = (zh * 2 + zl) * 2 + core
    for step in range(1, 16):
        there = rem(place + step, 16)
        pl.semaphore_signal(
            barrier,
            inc=1,
            device_id=device(zl_=rem(div(there, 2), 2), core_=rem(there, 2), zh_=div(there, 4)),
            device_id_type=MESH,
        )
    for to in (*y_to, x_up, x_down):
        pl.semaphore_signal(barrier, inc=1, device_id=to, device_id_type=MESH)
    from_zl = 1 - rem(div(x, 2) + rem(zh, 2), 2)
    from_x = rem(x + 2 * core + 1 - zl, RX)

    def from_here(half, q):
        return (x == from_x) & (zl == from_zl) & (core == half) & (zh == q)

    for half in range(2):
        for q in range(RZ):

            @pl.when(jnp.logical_not(from_here(half, q)))
            def _():
                pl.semaphore_signal(
                    barrier,
                    inc=1,
                    device_id=device(zl_=from_zl, core_=jnp.int32(half), x_=from_x, zh_=jnp.int32(q)),
                    device_id_type=MESH,
                )

    for load in loads:
        load.wait()
    for h in range(2):
        b_turned[h] = b_own[h].astype(F32).T.astype(BF16)
    pl.semaphore_wait(barrier, 27 - jnp.where((x == from_x) & (zl == from_zl), 1, 0))

    def ring_part(buf, owner, i):
        return buf.at[owner, pl.ds(i * HALF, HALF)]

    def ring_send(buf, s, r, way, hop, i):
        owner = rem(y + (RY - hop if way == 0 else hop), RY)
        send(ring_part(buf, owner, i), ring_part(buf, owner, i), s.at[way, hop, i], r.at[way, hop, i], y_to[way])

    def ring_wait(buf, r, way, hop, i):
        owner = rem(y + (RY - hop - 1 if way == 0 else hop + 1), RY)
        arrived(ring_part(buf, owner, i), r.at[way, hop, i])

    def ring_hop(buf, s, r, hop, parts=FAR_FIRST):
        for way, i in parts:
            ring_wait(buf, r, way, hop - 1, i)
            if hop < 3 or i // 2 == way:
                ring_send(buf, s, r, way, hop, i)

    def ring_end(buf, r):
        for way, i in FAR_FIRST:
            if i // 2 == way:
                ring_wait(buf, r, way, 3, i)

    def ring_sent(buf, s, hop):
        for way, i in FAR_FIRST:
            if hop < 3 or i // 2 == way:
                sent(ring_part(buf, 0, i), s.at[way, hop, i])

    for way, i in FAR_FIRST:
        ring_send(g_all, g_s, g_r, way, 0, i)

    b_here = rem(x, 2) * 4
    b_zl = div(x, 2)

    b_source = zl == b_zl
    b_first = rem(rem(x, 2) + rem(b_zl + zl, 2), 2) * 4

    for e in NEAR_ZH:
        to_zh = rem(zh + e, RZ)
        for h in range(2):

            def away():
                send(
                    b_turned.at[h], b_all.at[b_here + zh, own], bz_s.at[h, e], bz_r.at[own, zh],
                    device(zl_=b_zl, core_=jnp.int32(h), zh_=to_zh),
                )

            if e == 0:

                @pl.when(b_source & (core == h))
                def _():
                    b_all[b_here + zh, own] = b_turned[h]

                pl.when(jnp.logical_not(b_source & (core == h)))(away)
            else:
                away()

    def chunk(half, i):
        there = rem(2 * zh + zl + NEAR_Z[i], 2 * RZ)
        return b_all.at[half + div(there, 2), pl.ds(2 * rem(there, 2), 2)]

    def b_start(first, last):
        @pl.when(b_source)
        def _():
            for i in range(first, last):
                there = rem(2 * zh + zl + NEAR_Z[i], 2 * RZ)
                for c in range(2) if i > 0 else (1 - core,):
                    s = 2 * rem(there, 2) + c
                    arrived(b_all.at[b_here + div(there, 2), s], bz_r.at[s, div(there, 2)])
                block = chunk(b_here, i)
                send(block, block, bm_s.at[i], bm_r.at[i], x_mirror)
                send(block, block, bp_s.at[i], bp_r.at[i], x_pair)

    def b_forward(first, last):
        @pl.when(jnp.logical_not(b_source))
        def _():
            for i in range(first, last):
                block = chunk(b_first, i)
                arrived(block, bm_r.at[i])
                send(block, block, bp_s.at[i], bp_r.at[i], x_pair)

    b_start(0, 3)
    ring_hop(g_all, g_s, g_r, 1)
    b_start(3, 8)
    send(a_all.at[own], a_all.at[own], a_s.at[0], a_r.at[0], zl_other)
    send(a_all.at[own], a_all.at[own], a_s.at[1], a_r.at[1], core_other)
    b_forward(0, 3)
    ring_hop(g_all, g_s, g_r, 2)
    b_forward(3, 8)
    ring_hop(g_all, g_s, g_r, 3)
    ring_end(g_all, g_r)
    for i in range(2 * RZ):
        arrived(chunk(4 - b_first, i), bp_r.at[i])

    mine = rem(zl + y, 2)
    right = jnp.concatenate([b_all[:, t].reshape(RY * LANES, LANES) for t in range(4)], axis=1)
    for m in range(5):
        if m < 4:
            rows = pl.ds(m * HALF, HALF)
            left = jnp.concatenate([g_all[j, rows] for j in range(RY)], axis=1)
            share = jnp.dot(left, right, preferred_element_type=F32)
            for t in range(4):
                f_part[m, t] = share[:, t * LANES : (t + 1) * LANES]
            for t in range(2):
                c_out[m, t] = f_part[m, 2 * t + 1 - core].astype(BF16)
            send(c_out.at[m], c_in.at[m], c_s.at[m], c_r.at[m], core_other)
        if m >= 1:
            arrived(c_in.at[m - 1], c_r.at[m - 1])
            z_out[m - 1] = (
                f_part[m - 1, 2 * (1 - mine) + core] + c_in[m - 1, 1 - mine].astype(F32)
            ).astype(BF16)
            send(z_out.at[m - 1], z_in.at[m - 1], z_s.at[m - 1], z_r.at[m - 1], zl_other)
    a_next = a_all.at[2 * (1 - zl) + core]
    arrived(a_next, a_r.at[0])
    send(a_next, a_next, a_s.at[2], a_r.at[2], core_other)
    for m in range(4):
        arrived(z_in.at[m], z_r.at[m])
        h_all[y, pl.ds(m * HALF, HALF)] = (
            f_part[m, 2 * mine + core] + c_in[m, mine].astype(F32) + z_in[m].astype(F32)
        ).astype(BF16)
        for way in range(2):
            ring_send(h_all, h_s, h_r, way, 0, m)
    ring_hop(h_all, h_s, h_r, 1, AS_MADE[:2])
    arrived(a_all.at[2 * zl + 1 - core], a_r.at[1])
    arrived(a_all.at[2 * (1 - zl) + 1 - core], a_r.at[2])

    order = rem(y, 4)
    last = jnp.where(order == 0, 3, jnp.where(order == 3, 4, 5))
    steps = (
        (0,),
        (7, 1),
        (6, 2),
        (jnp.where((order == 0) | (order == 3), 5, 3), jnp.where(order == 3, 3, 4)),
        (last,),
    )

    def owner_x(o, plane):
        yy = rem(y + o, RY)
        return 2 * rem(plane + yy, 2) + div(yy, 4)

    def rows_at(o, at_x):
        away = rem(at_x + RX - owner_x(o, zl), RX)
        return 2 * (1 - rem(away, 2)) + div(away, 2)

    def multiply(step, s):
        offsets = steps[step]
        right = jnp.concatenate([h_all[rem(y + o, RY)] for o in offsets], axis=1)
        product = jnp.dot(a_all[s], right, preferred_element_type=F32).astype(BF16)
        for i, o in enumerate(offsets):
            to_x = rem(owner_x(o, zl) + 2 * rem(s, 2) + 1 - div(s, 2), RX)
            for half in range(2):
                part[step, to_x, half, i] = product[half * HALF : (half + 1) * HALF, i * LANES : (i + 1) * LANES]

    def count(step):
        return pl.ds(0, len(SLOTS[step]))

    s_up, s_down, s_far = rem(x + 1, RX), rem(x + RX - 1, RX), rem(x + 2, RX)

    def x_send(step):
        n = count(step)
        if len(SLOTS[step]) == 1:
            o = steps[step][0]
            multiply(step, rows_at(o, s_far))
        else:
            lax.fori_loop(0, 4, lambda i, carry: (multiply(step, i), carry)[1], 0)
        send(part.at[step, s_far, 0, n], relayed.at[step, 0, n], x_s.at[step, 0], rel_r.at[step, 0], x_down)
        send(part.at[step, s_far, 1, n], relayed.at[step, 1, n], x_s.at[step, 1], rel_r.at[step, 1], x_up)
        if len(SLOTS[step]) == 1:
            lax.fori_loop(3, 6, lambda i, carry: (multiply(step, rows_at(o, rem(x + i, RX))), carry)[1], 0)
        send(part.at[step, s_down, 1, n], x_in.at[step, 0, 1, n], x_s.at[step, 2], x_r.at[step, 0, 1], x_down)
        send(part.at[step, s_up, 0, n], x_in.at[step, 1, 0, n], x_s.at[step, 3], x_r.at[step, 1, 0], x_up)

    def x_relay(step):
        n = count(step)
        for half, s, to in ((0, s_down, x_down), (1, s_up, x_up)):
            arrived(relayed.at[step, half, n], rel_r.at[step, half])
            for i in range(len(SLOTS[step])):
                part[step, s, half, i] = (
                    part[step, s, half, i].astype(F32) + relayed[step, half, i].astype(F32)
                ).astype(BF16)
            send(
                part.at[step, s, half, n], x_in.at[step, half, half, n], x_s.at[step, 4 + half],
                x_r.at[step, half, half], to,
            )

    def z_send(step):
        n = count(step)
        for half in range(2):
            for side in range(2):
                arrived(x_in.at[step, side, half, n], x_r.at[step, side, half])
            for i in range(len(SLOTS[step])):
                total = (
                    part[step, x, half, i].astype(F32)
                    + x_in[step, 0, half, i].astype(F32)
                    + x_in[step, 1, half, i].astype(F32)
                ).astype(BF16)
                for q in range(2):
                    x_sum[step, 2 * half + q, i] = total[q * QUARTER : (q + 1) * QUARTER]
            for q in range(2 * half, 2 * half + 2):
                send(
                    x_sum.at[step, q, n], z_part.at[step, zh, n], zz_s.at[step, q], zz_r.at[step, zh],
                    device(zl_=1 - zl, zh_=jnp.int32(q)),
                )

    def owner(o):
        to_x = owner_x(o, 1 - zl)
        away = rem(x + RX - to_x, RX)
        return 1 - rem(away, 2), div(away, 2), to_x, rem(rem(y + o, RY), 4)

    def owned_here(o):
        to_zl, to_core, to_x, to_zh = owner(o)
        return (zl == to_zl) & (core == to_core) & (to_x == x) & (to_zh == zh)

    def piece(half, q):
        return out_ref.at[pl.ds(q * QUARTER, QUARTER), pl.ds(pl.multiple_of(half * LANES, LANES), LANES)]

    def last_send(step):
        n = count(step)
        for s in range(RZ):
            arrived(z_part.at[step, s, n], zz_r.at[step, s])
        for i, (slot, o) in enumerate(zip(SLOTS[step], steps[step])):
            total = z_part[step, 0, i].astype(F32)
            for s in range(1, RZ):
                total = total + z_part[step, s, i].astype(F32)
            z_sum[slot] = total.astype(BF16)
            to_zl, to_core, to_x, to_zh = owner(o)

            @pl.when(owned_here(o))
            def _():
                pltpu.make_async_copy(z_sum.at[slot], piece(core, zh), last_s.at[slot]).start()

            @pl.when(jnp.logical_not(owned_here(o)))
            def _():
                send(
                    z_sum.at[slot], piece(core, zh), last_s.at[slot], last_r.at[core, zh],
                    device(zl_=to_zl, core_=to_core, x_=to_x, zh_=to_zh),
                )

    def g_sent():
        for hop in range(4):
            ring_sent(g_all, g_s, hop)

    def b_sent():
        for e in NEAR_ZH:
            for h in range(2):

                def left_here():
                    sent(b_turned.at[h], bz_s.at[h, e])

                if e == 0:
                    pl.when(jnp.logical_not(b_source & (core == h)))(left_here)
                else:
                    left_here()

        for i in range(2 * RZ):
            sent(chunk(0, i), bp_s.at[i])

        @pl.when(b_source)
        def _():
            for i in range(2 * RZ):
                sent(chunk(0, i), bm_s.at[i])

    def a_sent():
        for i in range(3):
            sent(a_all.at[0], a_s.at[i])
        for m in range(4):
            sent(c_out.at[m], c_s.at[m])
            sent(z_out.at[m], z_s.at[m])
        ring_sent(h_all, h_s, 0)

    def steps_sent(step):
        n = count(step)
        for i in range(6):
            sent(part.at[step, 0, 0, n], x_s.at[step, i])
        for q in range(RZ):
            sent(x_sum.at[step, q, n], zz_s.at[step, q])

    def all_sent(step):
        if step == 0:
            g_sent()
        elif step == 1:
            b_sent()
        elif step == 2:
            a_sent()
        else:
            ring_sent(h_all, h_s, step - 2)
            steps_sent(step - 3)

    for step in range(len(SLOTS) + 2):
        if step == 3:
            ring_end(h_all, h_r)
        if step < len(SLOTS):
            x_send(step)
            if step < 3:
                ring_hop(h_all, h_s, h_r, step + 1, AS_MADE[2 if step == 0 else 0 :])
            all_sent(step)
            x_relay(step)
        for stage, back in ((z_send, 1), (last_send, 2)):
            if 0 <= step - back < len(SLOTS):
                stage(step - back)
        if step == 5:
            steps_sent(2)

    ring_sent(h_all, h_s, 3)
    steps_sent(3)
    steps_sent(4)
    for slot, o in enumerate(o for offsets in steps for o in offsets):

        @pl.when(owned_here(o))
        def _():
            pltpu.make_async_copy(z_sum.at[slot], piece(core, zh), last_s.at[slot]).wait()

        @pl.when(jnp.logical_not(owned_here(o)))
        def _():
            sent(z_sum.at[slot], last_s.at[slot])

    for half in range(2):
        for q in range(RZ):

            @pl.when(jnp.logical_not(from_here(half, q)))
            def _():
                arrived(piece(jnp.int32(half), jnp.int32(q)), last_r.at[half, q])


def body(out_inverse, gradient, in_inverse):
    dma = pltpu.SemaphoreType.DMA
    vmem = pltpu.VMEM
    return pl.pallas_call(
        kernel,
        out_shape=jax.ShapeDtypeStruct((ROWS, 2 * LANES), BF16),
        in_specs=[pl.BlockSpec(memory_space=pl.ANY)] * 3,
        out_specs=pl.BlockSpec(memory_space=pl.ANY),
        scratch_shapes=[
            vmem((4, ROWS, 2 * ROWS), BF16),
            vmem((RY, 2 * ROWS, LANES), BF16),
            vmem((2, LANES, LANES), BF16),
            vmem((2, LANES, LANES), BF16),
            vmem((RY, 4, LANES, LANES), BF16),
            vmem((4, 4, HALF, LANES), F32),
            vmem((4, 2, HALF, LANES), BF16),
            vmem((4, 2, HALF, LANES), BF16),
            vmem((4, HALF, LANES), BF16),
            vmem((4, HALF, LANES), BF16),
            vmem((RY, 2 * ROWS, LANES), BF16),
            vmem((5, 4, 2, 2, HALF, LANES), BF16),
            vmem((5, 2, 2, HALF, LANES), BF16),
            vmem((5, 2, 2, 2, HALF, LANES), BF16),
            vmem((5, RZ, 2, QUARTER, LANES), BF16),
            vmem((5, RZ, 2, QUARTER, LANES), BF16),
            vmem((RY, QUARTER, LANES), BF16),
            dma((4,)),
            dma((2, 4, 4)), dma((2, 4, 4)),
            dma((2, 4, 4)), dma((2, 4, 4)),
            dma((2, RZ)), dma((4, RZ)),
            dma((2 * RZ,)), dma((2 * RZ,)),
            dma((2 * RZ,)), dma((2 * RZ,)),
            dma((3,)), dma((3,)),
            dma((4,)), dma((4,)),
            dma((4,)), dma((4,)),
            dma((5, 6)), dma((5, 2)), dma((5, 2, 2)),
            dma((5, RZ)), dma((5, RZ)),
            dma((RY,)), dma((2, RZ)),
        ],
        compiler_params=pltpu.CompilerParams(
            collective_id=0, has_side_effects=True, vmem_limit_bytes=64 * 1024 * 1024
        ),
        cost_estimate=pl.CostEstimate(flops=4_300_000_000, bytes_accessed=2_000_000, transcendentals=0),
    )(out_inverse, gradient, in_inverse)


def solution(mesh):
    in_specs = (P("row", "col"), P("col", "row"), P("row", "col"))
    return jax.shard_map(body, mesh=mesh, in_specs=in_specs, out_specs=P("row", "col"), check_vma=False)
```

```python
import jax
import jax.numpy as jnp
from jax import lax
from jax.experimental import pallas as pl
from jax.experimental.pallas import tpu as pltpu
from jax.sharding import PartitionSpec as P

MESH = pl.DeviceIdType.MESH
BF16 = jnp.bfloat16
F32 = jnp.float32
RY, RX, RZ = 8, 4, 4
ROWS, HALF, QUARTER, LANES = 448, 224, 112, 128
SLOTS = ((0,), (1, 2), (3, 4), (5,), (6,), (7,))
NEAR_Z = (0, 1, 7, 2, 6, 3, 5, 4)
NEAR_ZH = (0, 1, 3, 2)
FAR_FIRST = ((0, 0), (1, 2), (0, 1), (1, 3), (0, 2), (1, 0), (0, 3), (1, 1))
AS_MADE = ((0, 0), (1, 0), (0, 1), (1, 1), (0, 2), (1, 2), (0, 3), (1, 3))


def rem(a, b):
    return lax.rem(a, jnp.int32(b))


def div(a, b):
    return lax.div(a, jnp.int32(b))


def kernel(
    a_ref, g_ref, b_ref, out_ref,
    a_all, g_all, b_own, b_turned, b_all, f_part, c_out, c_in, z_out, z_in, h_all, part, relayed, x_in, x_sum, z_part, z_sum,
    loc, g_s, g_r, h_s, h_r, bz_s, bz_r, bm_s, bm_r, bp_s, bp_r, a_s, a_r, c_s, c_r, z_s, z_r,
    x_s, rel_r, x_r, zz_s, zz_r, last_s, last_r,
):
    row, col = lax.axis_index("row"), lax.axis_index("col")
    core = rem(row, 2)
    y = rem(div(row, 2), RY)
    zl = div(row, 2 * RY)
    x, zh = div(col, RZ), rem(col, RZ)
    own = zl * 2 + core

    def device(zl_=zl, y_=y, core_=core, x_=x, zh_=zh):
        return ((zl_ * RY + y_) * 2 + core_, x_ * RZ + zh_)

    y_to = (device(y_=rem(y + 1, RY)), device(y_=rem(y + RY - 1, RY)))
    x_up, x_down = device(x_=rem(x + 1, RX)), device(x_=rem(x + RX - 1, RX))
    core_other, zl_other = device(core_=1 - core), device(zl_=1 - zl)
    x_pair, x_mirror = device(x_=x + 1 - 2 * rem(x, 2)), device(x_=RX - 1 - x)

    def remote(src, dst, send, recv, to):
        return pltpu.make_async_remote_copy(
            src_ref=src, dst_ref=dst, send_sem=send, recv_sem=recv, device_id=to, device_id_type=MESH
        )

    def send(src, dst, s, r, to):
        remote(src, dst, s, r, to).start()

    def sent(src, s):
        remote(src, src, s, s, core_other).wait_send()

    def arrived(dst, r):
        remote(dst, dst, r, r, core_other).wait_recv()

    loads = [
        pltpu.make_async_copy(g_ref, g_all.at[y], loc.at[0]),
        pltpu.make_async_copy(b_ref.at[:, pl.ds(0, LANES)], b_own.at[0], loc.at[1]),
        pltpu.make_async_copy(b_ref.at[:, pl.ds(LANES, LANES)], b_own.at[1], loc.at[2]),
        pltpu.make_async_copy(a_ref, a_all.at[own], loc.at[3]),
    ]
    for load in loads:
        load.start()
    barrier = pltpu.get_barrier_semaphore()
    for to in (*y_to, x_up, x_down):
        pl.semaphore_signal(barrier, inc=1, device_id=to, device_id_type=MESH)
    place = (zh * 2 + zl) * 2 + core
    for step in range(1, 16):
        there = rem(place + step, 16)
        pl.semaphore_signal(
            barrier,
            inc=1,
            device_id=device(zl_=rem(div(there, 2), 2), core_=rem(there, 2), zh_=div(there, 4)),
            device_id_type=MESH,
        )
    from_zl = 1 - rem(div(x, 2) + rem(zh, 2), 2)
    from_x = rem(x + 2 * core + 1 - zl, RX)

    def from_here(half, q):
        return (x == from_x) & (zl == from_zl) & (core == half) & (zh == q)

    for half in range(2):
        for q in range(RZ):

            @pl.when(jnp.logical_not(from_here(half, q)))
            def _():
                pl.semaphore_signal(
                    barrier,
                    inc=1,
                    device_id=device(zl_=from_zl, core_=jnp.int32(half), x_=from_x, zh_=jnp.int32(q)),
                    device_id_type=MESH,
                )

    for load in loads:
        load.wait()
    for h in range(2):
        b_turned[h] = b_own[h].astype(F32).T.astype(BF16)
    pl.semaphore_wait(barrier, 27 - jnp.where((x == from_x) & (zl == from_zl), 1, 0))

    def ring_part(buf, owner, i):
        return buf.at[owner, pl.ds(i * HALF, HALF)]

    def ring_send(buf, s, r, way, hop, i):
        owner = rem(y + (RY - hop if way == 0 else hop), RY)
        send(ring_part(buf, owner, i), ring_part(buf, owner, i), s.at[way, hop, i], r.at[way, hop, i], y_to[way])

    def ring_wait(buf, r, way, hop, i):
        owner = rem(y + (RY - hop - 1 if way == 0 else hop + 1), RY)
        arrived(ring_part(buf, owner, i), r.at[way, hop, i])

    def ring_hop(buf, s, r, hop, parts=FAR_FIRST):
        for way, i in parts:
            ring_wait(buf, r, way, hop - 1, i)
            if hop < 3 or i // 2 == way:
                ring_send(buf, s, r, way, hop, i)

    def ring_end(buf, r):
        for way, i in FAR_FIRST:
            if i // 2 == way:
                ring_wait(buf, r, way, 3, i)

    def ring_sent(buf, s, hop):
        for way, i in FAR_FIRST:
            if hop < 3 or i // 2 == way:
                sent(ring_part(buf, 0, i), s.at[way, hop, i])

    for way, i in FAR_FIRST:
        ring_send(g_all, g_s, g_r, way, 0, i)

    b_here = rem(x, 2) * 4
    b_zl = div(x, 2)

    b_source = zl == b_zl
    b_first = rem(rem(x, 2) + rem(b_zl + zl, 2), 2) * 4

    for e in NEAR_ZH:
        to_zh = rem(zh + e, RZ)
        for h in range(2):

            def away():
                send(
                    b_turned.at[h], b_all.at[b_here + zh, own], bz_s.at[h, e], bz_r.at[own, zh],
                    device(zl_=b_zl, core_=jnp.int32(h), zh_=to_zh),
                )

            if e == 0:

                @pl.when(b_source & (core == h))
                def _():
                    b_all[b_here + zh, own] = b_turned[h]

                pl.when(jnp.logical_not(b_source & (core == h)))(away)
            else:
                away()

    def chunk(half, i):
        there = rem(2 * zh + zl + NEAR_Z[i], 2 * RZ)
        return b_all.at[half + div(there, 2), pl.ds(2 * rem(there, 2), 2)]

    def b_start(first, last):
        @pl.when(b_source)
        def _():
            for i in range(first, last):
                there = rem(2 * zh + zl + NEAR_Z[i], 2 * RZ)
                for c in range(2) if i > 0 else (1 - core,):
                    s = 2 * rem(there, 2) + c
                    arrived(b_all.at[b_here + div(there, 2), s], bz_r.at[s, div(there, 2)])
                block = chunk(b_here, i)
                send(block, block, bm_s.at[i], bm_r.at[i], x_mirror)
                send(block, block, bp_s.at[i], bp_r.at[i], x_pair)

    def b_forward(first, last):
        @pl.when(jnp.logical_not(b_source))
        def _():
            for i in range(first, last):
                block = chunk(b_first, i)
                arrived(block, bm_r.at[i])
                send(block, block, bp_s.at[i], bp_r.at[i], x_pair)

    b_start(0, 3)
    ring_hop(g_all, g_s, g_r, 1)
    b_start(3, 8)
    send(a_all.at[own], a_all.at[own], a_s.at[0], a_r.at[0], zl_other)
    send(a_all.at[own], a_all.at[own], a_s.at[1], a_r.at[1], core_other)
    b_forward(0, 3)
    ring_hop(g_all, g_s, g_r, 2)
    b_forward(3, 8)
    ring_hop(g_all, g_s, g_r, 3)
    ring_end(g_all, g_r)
    for i in range(2 * RZ):
        arrived(chunk(4 - b_first, i), bp_r.at[i])

    mine = rem(zl + y, 2)
    right = jnp.concatenate([b_all[:, t].reshape(RY * LANES, LANES) for t in range(4)], axis=1)
    for m in range(5):
        if m < 4:
            rows = pl.ds(m * HALF, HALF)
            left = jnp.concatenate([g_all[j, rows] for j in range(RY)], axis=1)
            share = jnp.dot(left, right, preferred_element_type=F32)
            for t in range(4):
                f_part[m, t] = share[:, t * LANES : (t + 1) * LANES]
            for t in range(2):
                c_out[m, t] = f_part[m, 2 * t + 1 - core].astype(BF16)
            send(c_out.at[m], c_in.at[m], c_s.at[m], c_r.at[m], core_other)
        if m >= 1:
            arrived(c_in.at[m - 1], c_r.at[m - 1])
            z_out[m - 1] = (
                f_part[m - 1, 2 * (1 - mine) + core] + c_in[m - 1, 1 - mine].astype(F32)
            ).astype(BF16)
            send(z_out.at[m - 1], z_in.at[m - 1], z_s.at[m - 1], z_r.at[m - 1], zl_other)
    a_next = a_all.at[2 * (1 - zl) + core]
    arrived(a_next, a_r.at[0])
    send(a_next, a_next, a_s.at[2], a_r.at[2], core_other)
    for m in range(4):
        arrived(z_in.at[m], z_r.at[m])
        h_all[y, pl.ds(m * HALF, HALF)] = (
            f_part[m, 2 * mine + core] + c_in[m, mine].astype(F32) + z_in[m].astype(F32)
        ).astype(BF16)
        for way in range(2):
            ring_send(h_all, h_s, h_r, way, 0, m)
    ring_hop(h_all, h_s, h_r, 1, AS_MADE[:2])
    arrived(a_all.at[2 * zl + 1 - core], a_r.at[1])
    arrived(a_all.at[2 * (1 - zl) + 1 - core], a_r.at[2])

    order = rem(y, 4)
    steps = (
        (0,),
        (7, 1),
        (6, 2),
        (jnp.where(order == 0, 4, jnp.where(order == 3, 5, 3)),),
        (jnp.where(order == 0, 5, jnp.where(order == 3, 3, 4)),),
        (jnp.where(order == 0, 3, jnp.where(order == 3, 4, 5)),),
    )

    def owner_x(o, plane):
        yy = rem(y + o, RY)
        return 2 * rem(plane + yy, 2) + div(yy, 4)

    def rows_at(o, at_x):
        away = rem(at_x + RX - owner_x(o, zl), RX)
        return 2 * (1 - rem(away, 2)) + div(away, 2)

    def multiply(step, s):
        offsets = steps[step]
        right = jnp.concatenate([h_all[rem(y + o, RY)] for o in offsets], axis=1)
        product = jnp.dot(a_all[s], right, preferred_element_type=F32).astype(BF16)
        for i, o in enumerate(offsets):
            to_x = rem(owner_x(o, zl) + 2 * rem(s, 2) + 1 - div(s, 2), RX)
            for half in range(2):
                part[step, to_x, half, i] = product[half * HALF : (half + 1) * HALF, i * LANES : (i + 1) * LANES]

    def count(step):
        return pl.ds(0, len(SLOTS[step]))

    s_up, s_down, s_far = rem(x + 1, RX), rem(x + RX - 1, RX), rem(x + 2, RX)

    def x_send(step):
        n = count(step)
        if len(SLOTS[step]) == 1:
            o = steps[step][0]
            multiply(step, rows_at(o, s_far))
        else:
            lax.fori_loop(0, 4, lambda i, carry: (multiply(step, i), carry)[1], 0)
        send(part.at[step, s_far, 0, n], relayed.at[step, 0, n], x_s.at[step, 0], rel_r.at[step, 0], x_down)
        send(part.at[step, s_far, 1, n], relayed.at[step, 1, n], x_s.at[step, 1], rel_r.at[step, 1], x_up)
        if len(SLOTS[step]) == 1:
            lax.fori_loop(3, 6, lambda i, carry: (multiply(step, rows_at(o, rem(x + i, RX))), carry)[1], 0)
        send(part.at[step, s_down, 1, n], x_in.at[step, 0, 1, n], x_s.at[step, 2], x_r.at[step, 0, 1], x_down)
        send(part.at[step, s_up, 0, n], x_in.at[step, 1, 0, n], x_s.at[step, 3], x_r.at[step, 1, 0], x_up)

    def x_relay(step):
        n = count(step)
        for half, s, to in ((0, s_down, x_down), (1, s_up, x_up)):
            arrived(relayed.at[step, half, n], rel_r.at[step, half])
            for i in range(len(SLOTS[step])):
                part[step, s, half, i] = (
                    part[step, s, half, i].astype(F32) + relayed[step, half, i].astype(F32)
                ).astype(BF16)
            send(
                part.at[step, s, half, n], x_in.at[step, half, half, n], x_s.at[step, 4 + half],
                x_r.at[step, half, half], to,
            )

    def z_send(step):
        n = count(step)
        for half in range(2):
            for side in range(2):
                arrived(x_in.at[step, side, half, n], x_r.at[step, side, half])
            for i in range(len(SLOTS[step])):
                total = (
                    part[step, x, half, i].astype(F32)
                    + x_in[step, 0, half, i].astype(F32)
                    + x_in[step, 1, half, i].astype(F32)
                ).astype(BF16)
                for q in range(2):
                    x_sum[step, 2 * half + q, i] = total[q * QUARTER : (q + 1) * QUARTER]
            for q in range(2 * half, 2 * half + 2):
                send(
                    x_sum.at[step, q, n], z_part.at[step, zh, n], zz_s.at[step, q], zz_r.at[step, zh],
                    device(zl_=1 - zl, zh_=jnp.int32(q)),
                )

    def owner(o):
        to_x = owner_x(o, 1 - zl)
        away = rem(x + RX - to_x, RX)
        return 1 - rem(away, 2), div(away, 2), to_x, rem(rem(y + o, RY), 4)

    def owned_here(o):
        to_zl, to_core, to_x, to_zh = owner(o)
        return (zl == to_zl) & (core == to_core) & (to_x == x) & (to_zh == zh)

    def piece(half, q):
        return out_ref.at[pl.ds(q * QUARTER, QUARTER), pl.ds(pl.multiple_of(half * LANES, LANES), LANES)]

    def last_send(step):
        n = count(step)
        for s in range(RZ):
            arrived(z_part.at[step, s, n], zz_r.at[step, s])
        for i, (slot, o) in enumerate(zip(SLOTS[step], steps[step])):
            total = z_part[step, 0, i].astype(F32)
            for s in range(1, RZ):
                total = total + z_part[step, s, i].astype(F32)
            z_sum[slot] = total.astype(BF16)
            to_zl, to_core, to_x, to_zh = owner(o)

            @pl.when(owned_here(o))
            def _():
                pltpu.make_async_copy(z_sum.at[slot], piece(core, zh), last_s.at[slot]).start()

            @pl.when(jnp.logical_not(owned_here(o)))
            def _():
                send(
                    z_sum.at[slot], piece(core, zh), last_s.at[slot], last_r.at[core, zh],
                    device(zl_=to_zl, core_=to_core, x_=to_x, zh_=to_zh),
                )

    def g_sent():
        for hop in range(4):
            ring_sent(g_all, g_s, hop)

    def b_sent():
        for e in NEAR_ZH:
            for h in range(2):

                def left_here():
                    sent(b_turned.at[h], bz_s.at[h, e])

                if e == 0:
                    pl.when(jnp.logical_not(b_source & (core == h)))(left_here)
                else:
                    left_here()

        for i in range(2 * RZ):
            sent(chunk(0, i), bp_s.at[i])

        @pl.when(b_source)
        def _():
            for i in range(2 * RZ):
                sent(chunk(0, i), bm_s.at[i])

    def a_sent():
        for i in range(3):
            sent(a_all.at[0], a_s.at[i])
        for m in range(4):
            sent(c_out.at[m], c_s.at[m])
            sent(z_out.at[m], z_s.at[m])
        ring_sent(h_all, h_s, 0)

    def steps_sent(step):
        n = count(step)
        for i in range(6):
            sent(part.at[step, 0, 0, n], x_s.at[step, i])
        for q in range(RZ):
            sent(x_sum.at[step, q, n], zz_s.at[step, q])

    def all_sent(step):
        if step == 0:
            g_sent()
        elif step == 1:
            b_sent()
        elif step == 2:
            a_sent()
        else:
            if step < 5:
                ring_sent(h_all, h_s, step - 2)
            steps_sent(step - 3)

    for step in range(len(SLOTS) + 2):
        if step == 3:
            ring_end(h_all, h_r)
        if step < len(SLOTS):
            x_send(step)
            if step < 3:
                ring_hop(h_all, h_s, h_r, step + 1, AS_MADE[2 if step == 0 else 0 :])
            all_sent(step)
            x_relay(step)
        for stage, back in ((z_send, 1), (last_send, 2)):
            if 0 <= step - back < len(SLOTS):
                stage(step - back)

    ring_sent(h_all, h_s, 3)
    for step in range(3, 6):
        steps_sent(step)
    for slot, o in enumerate(o for offsets in steps for o in offsets):

        @pl.when(owned_here(o))
        def _():
            pltpu.make_async_copy(z_sum.at[slot], piece(core, zh), last_s.at[slot]).wait()

        @pl.when(jnp.logical_not(owned_here(o)))
        def _():
            sent(z_sum.at[slot], last_s.at[slot])

    for half in range(2):
        for q in range(RZ):

            @pl.when(jnp.logical_not(from_here(half, q)))
            def _():
                arrived(piece(jnp.int32(half), jnp.int32(q)), last_r.at[half, q])


def body(out_inverse, gradient, in_inverse):
    dma = pltpu.SemaphoreType.DMA
    vmem = pltpu.VMEM
    return pl.pallas_call(
        kernel,
        out_shape=jax.ShapeDtypeStruct((ROWS, 2 * LANES), BF16),
        in_specs=[pl.BlockSpec(memory_space=pl.ANY)] * 3,
        out_specs=pl.BlockSpec(memory_space=pl.ANY),
        scratch_shapes=[
            vmem((4, ROWS, 2 * ROWS), BF16),
            vmem((RY, 2 * ROWS, LANES), BF16),
            vmem((2, LANES, LANES), BF16),
            vmem((2, LANES, LANES), BF16),
            vmem((RY, 4, LANES, LANES), BF16),
            vmem((4, 4, HALF, LANES), F32),
            vmem((4, 2, HALF, LANES), BF16),
            vmem((4, 2, HALF, LANES), BF16),
            vmem((4, HALF, LANES), BF16),
            vmem((4, HALF, LANES), BF16),
            vmem((RY, 2 * ROWS, LANES), BF16),
            vmem((6, 4, 2, 2, HALF, LANES), BF16),
            vmem((6, 2, 2, HALF, LANES), BF16),
            vmem((6, 2, 2, 2, HALF, LANES), BF16),
            vmem((6, RZ, 2, QUARTER, LANES), BF16),
            vmem((6, RZ, 2, QUARTER, LANES), BF16),
            vmem((RY, QUARTER, LANES), BF16),
            dma((4,)),
            dma((2, 4, 4)), dma((2, 4, 4)),
            dma((2, 4, 4)), dma((2, 4, 4)),
            dma((2, RZ)), dma((4, RZ)),
            dma((2 * RZ,)), dma((2 * RZ,)),
            dma((2 * RZ,)), dma((2 * RZ,)),
            dma((3,)), dma((3,)),
            dma((4,)), dma((4,)),
            dma((4,)), dma((4,)),
            dma((6, 6)), dma((6, 2)), dma((6, 2, 2)),
            dma((6, RZ)), dma((6, RZ)),
            dma((RY,)), dma((2, RZ)),
        ],
        compiler_params=pltpu.CompilerParams(
            collective_id=0, has_side_effects=True, vmem_limit_bytes=64 * 1024 * 1024
        ),
        cost_estimate=pl.CostEstimate(flops=4_300_000_000, bytes_accessed=2_000_000, transcendentals=0),
    )(out_inverse, gradient, in_inverse)


def solution(mesh):
    in_specs = (P("row", "col"), P("col", "row"), P("row", "col"))
    return jax.shard_map(body, mesh=mesh, in_specs=in_specs, out_specs=P("row", "col"), check_vma=False)
```

```python
import jax
import jax.numpy as jnp
from jax import lax
from jax.experimental import pallas as pl
from jax.experimental.pallas import tpu as pltpu
from jax.sharding import PartitionSpec as P

MESH = pl.DeviceIdType.MESH
BF16 = jnp.bfloat16
F32 = jnp.float32
RY, RX, RZ = 8, 4, 4
ROWS, HALF, QUARTER, LANES = 448, 224, 112, 128
SLOTS = ((0,), (1, 2), (3, 4), (5, 6), (7,))
NEAR_Z = (0, 1, 7, 2, 6, 3, 5, 4)
NEAR_ZH = (0, 1, 3, 2)
FAR_FIRST = ((0, 0), (1, 2), (0, 1), (1, 3), (0, 2), (1, 0), (0, 3), (1, 1))
AS_MADE = ((0, 0), (1, 0), (0, 1), (1, 1), (0, 2), (1, 2), (0, 3), (1, 3))


def rem(a, b):
    return lax.rem(a, jnp.int32(b))


def div(a, b):
    return lax.div(a, jnp.int32(b))


def kernel(
    a_ref, g_ref, b_ref, out_ref,
    a_all, g_all, b_own, b_turned, b_all, f_part, c_out, c_in, z_out, z_in, h_all, part, relayed, x_in, x_sum, z_part, z_sum,
    loc, g_s, g_r, h_s, h_r, bz_s, bz_r, bm_s, bm_r, bp_s, bp_r, a_s, a_r, c_s, c_r, z_s, z_r,
    x_s, rel_r, x_r, zz_s, zz_r, last_s, last_r,
):
    row, col = lax.axis_index("row"), lax.axis_index("col")
    core = rem(row, 2)
    y = rem(div(row, 2), RY)
    zl = div(row, 2 * RY)
    x, zh = div(col, RZ), rem(col, RZ)
    own = zl * 2 + core

    def device(zl_=zl, y_=y, core_=core, x_=x, zh_=zh):
        return ((zl_ * RY + y_) * 2 + core_, x_ * RZ + zh_)

    y_to = (device(y_=rem(y + 1, RY)), device(y_=rem(y + RY - 1, RY)))
    x_up, x_down = device(x_=rem(x + 1, RX)), device(x_=rem(x + RX - 1, RX))
    core_other, zl_other = device(core_=1 - core), device(zl_=1 - zl)
    x_pair, x_mirror = device(x_=x + 1 - 2 * rem(x, 2)), device(x_=RX - 1 - x)

    def remote(src, dst, send, recv, to):
        return pltpu.make_async_remote_copy(
            src_ref=src, dst_ref=dst, send_sem=send, recv_sem=recv, device_id=to, device_id_type=MESH
        )

    def send(src, dst, s, r, to):
        remote(src, dst, s, r, to).start()

    def sent(src, s):
        remote(src, src, s, s, core_other).wait_send()

    def arrived(dst, r):
        remote(dst, dst, r, r, core_other).wait_recv()

    loads = [
        pltpu.make_async_copy(g_ref, g_all.at[y], loc.at[0]),
        pltpu.make_async_copy(b_ref.at[:, pl.ds(0, LANES)], b_own.at[0], loc.at[1]),
        pltpu.make_async_copy(b_ref.at[:, pl.ds(LANES, LANES)], b_own.at[1], loc.at[2]),
        pltpu.make_async_copy(a_ref, a_all.at[own], loc.at[3]),
    ]
    for load in loads:
        load.start()
    barrier = pltpu.get_barrier_semaphore()
    place = (zh * 2 + zl) * 2 + core
    for step in range(1, 16):
        there = rem(place + step, 16)
        pl.semaphore_signal(
            barrier,
            inc=1,
            device_id=device(zl_=rem(div(there, 2), 2), core_=rem(there, 2), zh_=div(there, 4)),
            device_id_type=MESH,
        )
    for to in (*y_to, x_up, x_down):
        pl.semaphore_signal(barrier, inc=1, device_id=to, device_id_type=MESH)
    from_zl = 1 - rem(div(x, 2) + rem(zh, 2), 2)
    from_x = rem(x + 2 * core + 1 - zl, RX)

    def from_here(half, q):
        return (x == from_x) & (zl == from_zl) & (core == half) & (zh == q)

    for half in range(2):
        for q in range(RZ):

            @pl.when(jnp.logical_not(from_here(half, q)))
            def _():
                pl.semaphore_signal(
                    barrier,
                    inc=1,
                    device_id=device(zl_=from_zl, core_=jnp.int32(half), x_=from_x, zh_=jnp.int32(q)),
                    device_id_type=MESH,
                )

    for load in loads:
        load.wait()
    for h in range(2):
        b_turned[h] = b_own[h].astype(F32).T.astype(BF16)
    pl.semaphore_wait(barrier, 27 - jnp.where((x == from_x) & (zl == from_zl), 1, 0))

    def ring_part(buf, owner, i):
        return buf.at[owner, pl.ds(i * HALF, HALF)]

    def ring_send(buf, s, r, way, hop, i):
        owner = rem(y + (RY - hop if way == 0 else hop), RY)
        send(ring_part(buf, owner, i), ring_part(buf, owner, i), s.at[way, hop, i], r.at[way, hop, i], y_to[way])

    def ring_wait(buf, r, way, hop, i):
        owner = rem(y + (RY - hop - 1 if way == 0 else hop + 1), RY)
        arrived(ring_part(buf, owner, i), r.at[way, hop, i])

    def ring_hop(buf, s, r, hop, parts=FAR_FIRST):
        for way, i in parts:
            ring_wait(buf, r, way, hop - 1, i)
            if hop < 3 or i // 2 == way:
                ring_send(buf, s, r, way, hop, i)

    def ring_end(buf, r):
        for way, i in FAR_FIRST:
            if i // 2 == way:
                ring_wait(buf, r, way, 3, i)

    def ring_sent(buf, s, hop):
        for way, i in FAR_FIRST:
            if hop < 3 or i // 2 == way:
                sent(ring_part(buf, 0, i), s.at[way, hop, i])

    def g_start(k):
        for way, i in FAR_FIRST[2 * k - 2 : 2 * k] if k > 0 else ():
            sent(ring_part(g_all, 0, i), g_s.at[way, 0, i])
        for way, i in FAR_FIRST[2 * k : 2 * k + 2]:
            ring_send(g_all, g_s, g_r, way, 0, i)

    def g_step(hop, k):
        ring_hop(g_all, g_s, g_r, hop, FAR_FIRST[2 * k : 2 * k + 2])

    g_start(0)

    b_here = rem(x, 2) * 4
    b_zl = div(x, 2)

    b_source = zl == b_zl
    b_first = rem(rem(x, 2) + rem(b_zl + zl, 2), 2) * 4

    for e in NEAR_ZH:
        to_zh = rem(zh + e, RZ)
        for h in range(2):

            def away():
                send(
                    b_turned.at[h], b_all.at[b_here + zh, own], bz_s.at[h, e], bz_r.at[own, zh],
                    device(zl_=b_zl, core_=jnp.int32(h), zh_=to_zh),
                )

            if e == 0:

                @pl.when(b_source & (core == h))
                def _():
                    b_all[b_here + zh, own] = b_turned[h]

                pl.when(jnp.logical_not(b_source & (core == h)))(away)
            else:
                away()

    def chunk(half, i):
        there = rem(2 * zh + zl + NEAR_Z[i], 2 * RZ)
        return b_all.at[half + div(there, 2), pl.ds(2 * rem(there, 2), 2)]

    def b_start(first, last):
        @pl.when(b_source)
        def _():
            for i in range(first, last):
                there = rem(2 * zh + zl + NEAR_Z[i], 2 * RZ)
                for c in range(2) if i > 0 else (1 - core,):
                    s = 2 * rem(there, 2) + c
                    arrived(b_all.at[b_here + div(there, 2), s], bz_r.at[s, div(there, 2)])
                block = chunk(b_here, i)
                send(block, block, bm_s.at[i], bm_r.at[i], x_mirror)
                send(block, block, bp_s.at[i], bp_r.at[i], x_pair)

    def b_forward(first, last):
        @pl.when(jnp.logical_not(b_source))
        def _():
            for i in range(first, last):
                block = chunk(b_first, i)
                arrived(block, bm_r.at[i])
                send(block, block, bp_s.at[i], bp_r.at[i], x_pair)

    for i in range(3):
        g_start(i + 1)
        b_start(i, i + 1)
    g_start(4)
    ring_hop(g_all, g_s, g_r, 1)
    b_start(3, 4)
    send(a_all.at[own], a_all.at[own], a_s.at[0], a_r.at[0], zl_other)
    send(a_all.at[own], a_all.at[own], a_s.at[1], a_r.at[1], core_other)
    b_forward(0, 2)
    g_step(2, 0)
    b_start(4, 5)
    b_forward(2, 3)
    g_step(2, 1)
    b_start(5, 6)
    g_step(2, 2)
    b_start(6, 7)
    b_forward(3, 4)
    g_step(2, 3)
    b_start(7, 8)
    b_forward(4, 5)
    for k in range(3):
        g_step(3, k)
        b_forward(5 + k, 6 + k)
    g_step(3, 3)
    ring_end(g_all, g_r)
    for i in range(2 * RZ):
        arrived(chunk(4 - b_first, i), bp_r.at[i])

    mine = rem(zl + y, 2)
    right = jnp.concatenate([b_all[:, t].reshape(RY * LANES, LANES) for t in range(4)], axis=1)
    for m in range(5):
        if m < 4:
            rows = pl.ds(m * HALF, HALF)
            left = jnp.concatenate([g_all[j, rows] for j in range(RY)], axis=1)
            share = jnp.dot(left, right, preferred_element_type=F32)
            for t in range(4):
                f_part[m, t] = share[:, t * LANES : (t + 1) * LANES]
            for t in range(2):
                c_out[m, t] = f_part[m, 2 * t + 1 - core].astype(BF16)
            send(c_out.at[m], c_in.at[m], c_s.at[m], c_r.at[m], core_other)
        if m >= 1:
            arrived(c_in.at[m - 1], c_r.at[m - 1])
            z_out[m - 1] = (
                f_part[m - 1, 2 * (1 - mine) + core] + c_in[m - 1, 1 - mine].astype(F32)
            ).astype(BF16)
            send(z_out.at[m - 1], z_in.at[m - 1], z_s.at[m - 1], z_r.at[m - 1], zl_other)
    a_next = a_all.at[2 * (1 - zl) + core]
    arrived(a_next, a_r.at[0])
    send(a_next, a_next, a_s.at[2], a_r.at[2], core_other)
    for m in range(4):
        arrived(z_in.at[m], z_r.at[m])
        h_all[y, pl.ds(m * HALF, HALF)] = (
            f_part[m, 2 * mine + core] + c_in[m, mine].astype(F32) + z_in[m].astype(F32)
        ).astype(BF16)
        for way in range(2):
            ring_send(h_all, h_s, h_r, way, 0, m)
    ring_hop(h_all, h_s, h_r, 1, AS_MADE[:2])
    arrived(a_all.at[2 * zl + 1 - core], a_r.at[1])
    arrived(a_all.at[2 * (1 - zl) + 1 - core], a_r.at[2])

    order = rem(y, 4)
    last = jnp.where(order == 0, 3, jnp.where(order == 3, 4, 5))
    steps = (
        (0,),
        (7, 1),
        (6, 2),
        (jnp.where((order == 0) | (order == 3), 5, 3), jnp.where(order == 3, 3, 4)),
        (last,),
    )

    def owner_x(o, plane):
        yy = rem(y + o, RY)
        return 2 * rem(plane + yy, 2) + div(yy, 4)

    def rows_at(o, at_x):
        away = rem(at_x + RX - owner_x(o, zl), RX)
        return 2 * (1 - rem(away, 2)) + div(away, 2)

    def multiply(step, s):
        offsets = steps[step]
        right = jnp.concatenate([h_all[rem(y + o, RY)] for o in offsets], axis=1)
        product = jnp.dot(a_all[s], right, preferred_element_type=F32).astype(BF16)
        for i, o in enumerate(offsets):
            to_x = rem(owner_x(o, zl) + 2 * rem(s, 2) + 1 - div(s, 2), RX)
            for half in range(2):
                part[step, to_x, half, i] = product[half * HALF : (half + 1) * HALF, i * LANES : (i + 1) * LANES]

    def count(step):
        return pl.ds(0, len(SLOTS[step]))

    s_up, s_down, s_far = rem(x + 1, RX), rem(x + RX - 1, RX), rem(x + 2, RX)

    def x_send(step):
        n = count(step)
        if len(SLOTS[step]) == 1:
            o = steps[step][0]
            multiply(step, rows_at(o, s_far))
        else:
            lax.fori_loop(0, 4, lambda i, carry: (multiply(step, i), carry)[1], 0)
        send(part.at[step, s_far, 0, n], relayed.at[step, 0, n], x_s.at[step, 0], rel_r.at[step, 0], x_down)
        send(part.at[step, s_far, 1, n], relayed.at[step, 1, n], x_s.at[step, 1], rel_r.at[step, 1], x_up)
        if len(SLOTS[step]) == 1:
            lax.fori_loop(3, 6, lambda i, carry: (multiply(step, rows_at(o, rem(x + i, RX))), carry)[1], 0)
        send(part.at[step, s_down, 1, n], x_in.at[step, 0, 1, n], x_s.at[step, 2], x_r.at[step, 0, 1], x_down)
        send(part.at[step, s_up, 0, n], x_in.at[step, 1, 0, n], x_s.at[step, 3], x_r.at[step, 1, 0], x_up)

    def x_relay(step):
        n = count(step)
        for half, s, to in ((0, s_down, x_down), (1, s_up, x_up)):
            arrived(relayed.at[step, half, n], rel_r.at[step, half])
            for i in range(len(SLOTS[step])):
                part[step, s, half, i] = (
                    part[step, s, half, i].astype(F32) + relayed[step, half, i].astype(F32)
                ).astype(BF16)
            send(
                part.at[step, s, half, n], x_in.at[step, half, half, n], x_s.at[step, 4 + half],
                x_r.at[step, half, half], to,
            )

    def z_send(step):
        n = count(step)
        for half in range(2):
            for side in range(2):
                arrived(x_in.at[step, side, half, n], x_r.at[step, side, half])
            for i in range(len(SLOTS[step])):
                total = (
                    part[step, x, half, i].astype(F32)
                    + x_in[step, 0, half, i].astype(F32)
                    + x_in[step, 1, half, i].astype(F32)
                ).astype(BF16)
                for q in range(2):
                    x_sum[step, 2 * half + q, i] = total[q * QUARTER : (q + 1) * QUARTER]
            for q in range(2 * half, 2 * half + 2):
                send(
                    x_sum.at[step, q, n], z_part.at[step, zh, n], zz_s.at[step, q], zz_r.at[step, zh],
                    device(zl_=1 - zl, zh_=jnp.int32(q)),
                )

    def owner(o):
        to_x = owner_x(o, 1 - zl)
        away = rem(x + RX - to_x, RX)
        return 1 - rem(away, 2), div(away, 2), to_x, rem(rem(y + o, RY), 4)

    def owned_here(o):
        to_zl, to_core, to_x, to_zh = owner(o)
        return (zl == to_zl) & (core == to_core) & (to_x == x) & (to_zh == zh)

    def piece(half, q):
        return out_ref.at[pl.ds(q * QUARTER, QUARTER), pl.ds(pl.multiple_of(half * LANES, LANES), LANES)]

    def last_send(step):
        n = count(step)
        for s in range(RZ):
            arrived(z_part.at[step, s, n], zz_r.at[step, s])
        for i, (slot, o) in enumerate(zip(SLOTS[step], steps[step])):
            total = z_part[step, 0, i].astype(F32)
            for s in range(1, RZ):
                total = total + z_part[step, s, i].astype(F32)
            z_sum[slot] = total.astype(BF16)
            to_zl, to_core, to_x, to_zh = owner(o)

            @pl.when(owned_here(o))
            def _():
                pltpu.make_async_copy(z_sum.at[slot], piece(core, zh), last_s.at[slot]).start()

            @pl.when(jnp.logical_not(owned_here(o)))
            def _():
                send(
                    z_sum.at[slot], piece(core, zh), last_s.at[slot], last_r.at[core, zh],
                    device(zl_=to_zl, core_=to_core, x_=to_x, zh_=to_zh),
                )

    def g_sent():
        for hop in range(1, 4):
            ring_sent(g_all, g_s, hop)

    def b_sent():
        for e in NEAR_ZH:
            for h in range(2):

                def left_here():
                    sent(b_turned.at[h], bz_s.at[h, e])

                if e == 0:
                    pl.when(jnp.logical_not(b_source & (core == h)))(left_here)
                else:
                    left_here()

        for i in range(2 * RZ):
            sent(chunk(0, i), bp_s.at[i])

        @pl.when(b_source)
        def _():
            for i in range(2 * RZ):
                sent(chunk(0, i), bm_s.at[i])

    def a_sent():
        for i in range(3):
            sent(a_all.at[0], a_s.at[i])
        for m in range(4):
            sent(c_out.at[m], c_s.at[m])
            sent(z_out.at[m], z_s.at[m])
        ring_sent(h_all, h_s, 0)

    def steps_sent(step):
        n = count(step)
        for i in range(6):
            sent(part.at[step, 0, 0, n], x_s.at[step, i])
        for q in range(RZ):
            sent(x_sum.at[step, q, n], zz_s.at[step, q])

    def all_sent(step):
        if step == 0:
            g_sent()
        elif step == 1:
            b_sent()
        elif step == 2:
            a_sent()
        else:
            ring_sent(h_all, h_s, step - 2)
            steps_sent(step - 3)

    for step in range(len(SLOTS) + 2):
        if step == 3:
            ring_end(h_all, h_r)
        if step < len(SLOTS):
            x_send(step)
            if step < 3:
                ring_hop(h_all, h_s, h_r, step + 1, AS_MADE[2 if step == 0 else 0 :])
            all_sent(step)
            x_relay(step)
        for stage, back in ((z_send, 1), (last_send, 2)):
            if 0 <= step - back < len(SLOTS):
                stage(step - back)
        if step == 5:
            steps_sent(2)

    ring_sent(h_all, h_s, 3)
    steps_sent(3)
    steps_sent(4)
    for slot, o in enumerate(o for offsets in steps for o in offsets):

        @pl.when(owned_here(o))
        def _():
            pltpu.make_async_copy(z_sum.at[slot], piece(core, zh), last_s.at[slot]).wait()

        @pl.when(jnp.logical_not(owned_here(o)))
        def _():
            sent(z_sum.at[slot], last_s.at[slot])

    for half in range(2):
        for q in range(RZ):

            @pl.when(jnp.logical_not(from_here(half, q)))
            def _():
                arrived(piece(jnp.int32(half), jnp.int32(q)), last_r.at[half, q])


def body(out_inverse, gradient, in_inverse):
    dma = pltpu.SemaphoreType.DMA
    vmem = pltpu.VMEM
    return pl.pallas_call(
        kernel,
        out_shape=jax.ShapeDtypeStruct((ROWS, 2 * LANES), BF16),
        in_specs=[pl.BlockSpec(memory_space=pl.ANY)] * 3,
        out_specs=pl.BlockSpec(memory_space=pl.ANY),
        scratch_shapes=[
            vmem((4, ROWS, 2 * ROWS), BF16),
            vmem((RY, 2 * ROWS, LANES), BF16),
            vmem((2, LANES, LANES), BF16),
            vmem((2, LANES, LANES), BF16),
            vmem((RY, 4, LANES, LANES), BF16),
            vmem((4, 4, HALF, LANES), F32),
            vmem((4, 2, HALF, LANES), BF16),
            vmem((4, 2, HALF, LANES), BF16),
            vmem((4, HALF, LANES), BF16),
            vmem((4, HALF, LANES), BF16),
            vmem((RY, 2 * ROWS, LANES), BF16),
            vmem((5, 4, 2, 2, HALF, LANES), BF16),
            vmem((5, 2, 2, HALF, LANES), BF16),
            vmem((5, 2, 2, 2, HALF, LANES), BF16),
            vmem((5, RZ, 2, QUARTER, LANES), BF16),
            vmem((5, RZ, 2, QUARTER, LANES), BF16),
            vmem((RY, QUARTER, LANES), BF16),
            dma((4,)),
            dma((2, 4, 4)), dma((2, 4, 4)),
            dma((2, 4, 4)), dma((2, 4, 4)),
            dma((2, RZ)), dma((4, RZ)),
            dma((2 * RZ,)), dma((2 * RZ,)),
            dma((2 * RZ,)), dma((2 * RZ,)),
            dma((3,)), dma((3,)),
            dma((4,)), dma((4,)),
            dma((4,)), dma((4,)),
            dma((5, 6)), dma((5, 2)), dma((5, 2, 2)),
            dma((5, RZ)), dma((5, RZ)),
            dma((RY,)), dma((2, RZ)),
        ],
        compiler_params=pltpu.CompilerParams(
            collective_id=0, has_side_effects=True, vmem_limit_bytes=64 * 1024 * 1024
        ),
        cost_estimate=pl.CostEstimate(flops=4_300_000_000, bytes_accessed=2_000_000, transcendentals=0),
    )(out_inverse, gradient, in_inverse)


def solution(mesh):
    in_specs = (P("row", "col"), P("col", "row"), P("row", "col"))
    return jax.shard_map(body, mesh=mesh, in_specs=in_specs, out_specs=P("row", "col"), check_vma=False)
```

```python
import jax
import jax.numpy as jnp
from jax import lax
from jax.experimental import pallas as pl
from jax.experimental.pallas import tpu as pltpu
from jax.sharding import PartitionSpec as P

MESH = pl.DeviceIdType.MESH
BF16 = jnp.bfloat16
F32 = jnp.float32
RY, RX, RZ = 8, 4, 4
ROWS, HALF, QUARTER, LANES = 448, 224, 112, 128
SLOTS = ((0,), (1, 2), (3, 4), (5, 6), (7,))
NEAR_Z = (0, 1, 7, 2, 6, 3, 5, 4)
NEAR_ZH = (0, 1, 3, 2)
FAR_FIRST = ((0, 0), (1, 2), (0, 1), (1, 3), (0, 2), (1, 0), (0, 3), (1, 1))
AS_MADE = ((0, 0), (1, 0), (0, 1), (1, 1), (0, 2), (1, 2), (0, 3), (1, 3))


def rem(a, b):
    return lax.rem(a, jnp.int32(b))


def div(a, b):
    return lax.div(a, jnp.int32(b))


def kernel(
    a_ref, g_ref, b_ref, out_ref,
    a_all, g_all, b_own, b_turned, b_all, f_part, c_out, c_in, z_out, z_in, h_all, part, relayed, x_in, x_sum, z_part, z_sum,
    loc, g_s, g_r, h_s, h_r, bz_s, bz_r, bm_s, bm_r, bp_s, bp_r, a_s, a_r, c_s, c_r, z_s, z_r,
    x_s, rel_r, x_r, zz_s, zz_r, last_s, last_r,
):
    row, col = lax.axis_index("row"), lax.axis_index("col")
    core = rem(row, 2)
    y = rem(div(row, 2), RY)
    zl = div(row, 2 * RY)
    x, zh = div(col, RZ), rem(col, RZ)
    own = zl * 2 + core

    def device(zl_=zl, y_=y, core_=core, x_=x, zh_=zh):
        return ((zl_ * RY + y_) * 2 + core_, x_ * RZ + zh_)

    y_to = (device(y_=rem(y + 1, RY)), device(y_=rem(y + RY - 1, RY)))
    x_up, x_down = device(x_=rem(x + 1, RX)), device(x_=rem(x + RX - 1, RX))
    core_other, zl_other = device(core_=1 - core), device(zl_=1 - zl)
    x_pair, x_mirror = device(x_=x + 1 - 2 * rem(x, 2)), device(x_=RX - 1 - x)

    def remote(src, dst, send, recv, to):
        return pltpu.make_async_remote_copy(
            src_ref=src, dst_ref=dst, send_sem=send, recv_sem=recv, device_id=to, device_id_type=MESH
        )

    def send(src, dst, s, r, to):
        remote(src, dst, s, r, to).start()

    def sent(src, s):
        remote(src, src, s, s, core_other).wait_send()

    def arrived(dst, r):
        remote(dst, dst, r, r, core_other).wait_recv()

    loads = [
        pltpu.make_async_copy(g_ref, g_all.at[y], loc.at[0]),
        pltpu.make_async_copy(b_ref.at[:, pl.ds(0, LANES)], b_own.at[0], loc.at[1]),
        pltpu.make_async_copy(b_ref.at[:, pl.ds(LANES, LANES)], b_own.at[1], loc.at[2]),
        pltpu.make_async_copy(a_ref, a_all.at[own], loc.at[3]),
    ]
    for load in loads:
        load.start()
    barrier = pltpu.get_barrier_semaphore()
    for to in (*y_to, x_up, x_down):
        pl.semaphore_signal(barrier, inc=1, device_id=to, device_id_type=MESH)
    place = (zh * 2 + zl) * 2 + core
    for step in range(1, 16):
        there = rem(place + step, 16)
        pl.semaphore_signal(
            barrier,
            inc=1,
            device_id=device(zl_=rem(div(there, 2), 2), core_=rem(there, 2), zh_=div(there, 4)),
            device_id_type=MESH,
        )
    from_zl = 1 - rem(div(x, 2) + rem(zh, 2), 2)
    from_x = rem(x + 2 * core + 1 - zl, RX)

    def from_here(half, q):
        return (x == from_x) & (zl == from_zl) & (core == half) & (zh == q)

    for half in range(2):
        for q in range(RZ):

            @pl.when(jnp.logical_not(from_here(half, q)))
            def _():
                pl.semaphore_signal(
                    barrier,
                    inc=1,
                    device_id=device(zl_=from_zl, core_=jnp.int32(half), x_=from_x, zh_=jnp.int32(q)),
                    device_id_type=MESH,
                )

    for load in loads:
        load.wait()
    for h in range(2):
        b_turned[h] = b_own[h].astype(F32).T.astype(BF16)
    pl.semaphore_wait(barrier, 27 - jnp.where((x == from_x) & (zl == from_zl), 1, 0))

    def ring_part(buf, owner, i):
        return buf.at[owner, pl.ds(i * HALF, HALF)]

    def ring_send(buf, s, r, way, hop, i):
        owner = rem(y + (RY - hop if way == 0 else hop), RY)
        send(ring_part(buf, owner, i), ring_part(buf, owner, i), s.at[way, hop, i], r.at[way, hop, i], y_to[way])

    def ring_wait(buf, r, way, hop, i):
        owner = rem(y + (RY - hop - 1 if way == 0 else hop + 1), RY)
        arrived(ring_part(buf, owner, i), r.at[way, hop, i])

    def ring_hop(buf, s, r, hop, parts=FAR_FIRST):
        for way, i in parts:
            ring_wait(buf, r, way, hop - 1, i)
            if hop < 3 or i // 2 == way:
                ring_send(buf, s, r, way, hop, i)

    def ring_end(buf, r):
        for way, i in FAR_FIRST:
            if i // 2 == way:
                ring_wait(buf, r, way, 3, i)

    def ring_sent(buf, s, hop):
        for way, i in FAR_FIRST:
            if hop < 3 or i // 2 == way:
                sent(ring_part(buf, 0, i), s.at[way, hop, i])

    for way, i in FAR_FIRST:
        ring_send(g_all, g_s, g_r, way, 0, i)

    b_here = rem(x, 2) * 4
    b_zl = div(x, 2)

    b_source = zl == b_zl
    b_first = rem(rem(x, 2) + rem(b_zl + zl, 2), 2) * 4

    for e in NEAR_ZH:
        to_zh = rem(zh + e, RZ)
        for h in range(2):

            def away():
                send(
                    b_turned.at[h], b_all.at[b_here + zh, own], bz_s.at[h, e], bz_r.at[own, zh],
                    device(zl_=b_zl, core_=jnp.int32(h), zh_=to_zh),
                )

            if e == 0:

                @pl.when(b_source & (core == h))
                def _():
                    b_all[b_here + zh, own] = b_turned[h]

                pl.when(jnp.logical_not(b_source & (core == h)))(away)
            else:
                away()

    def chunk(half, i):
        there = rem(2 * zh + zl + NEAR_Z[i], 2 * RZ)
        return b_all.at[half + div(there, 2), pl.ds(2 * rem(there, 2), 2)]

    def b_start(first, last):
        @pl.when(b_source)
        def _():
            for i in range(first, last):
                there = rem(2 * zh + zl + NEAR_Z[i], 2 * RZ)
                for c in range(2) if i > 0 else (1 - core,):
                    s = 2 * rem(there, 2) + c
                    arrived(b_all.at[b_here + div(there, 2), s], bz_r.at[s, div(there, 2)])
                block = chunk(b_here, i)
                send(block, block, bm_s.at[i], bm_r.at[i], x_mirror)
                send(block, block, bp_s.at[i], bp_r.at[i], x_pair)

    def b_forward(first, last):
        @pl.when(jnp.logical_not(b_source))
        def _():
            for i in range(first, last):
                block = chunk(b_first, i)
                arrived(block, bm_r.at[i])
                send(block, block, bp_s.at[i], bp_r.at[i], x_pair)

    b_start(0, 3)
    ring_hop(g_all, g_s, g_r, 1)
    b_start(3, 8)
    send(a_all.at[own], a_all.at[own], a_s.at[0], a_r.at[0], zl_other)
    send(a_all.at[own], a_all.at[own], a_s.at[1], a_r.at[1], core_other)
    b_forward(0, 3)
    ring_hop(g_all, g_s, g_r, 2)
    b_forward(3, 8)
    ring_hop(g_all, g_s, g_r, 3)
    ring_end(g_all, g_r)
    for i in range(2 * RZ):
        arrived(chunk(4 - b_first, i), bp_r.at[i])

    mine = rem(zl + y, 2)
    right = jnp.concatenate([b_all[:, t].reshape(RY * LANES, LANES) for t in range(4)], axis=1)
    for m in range(5):
        if m < 4:
            rows = pl.ds(m * HALF, HALF)
            left = jnp.concatenate([g_all[j, rows] for j in range(RY)], axis=1)
            share = jnp.dot(left, right, preferred_element_type=F32)
            for t in range(4):
                f_part[m, t] = share[:, t * LANES : (t + 1) * LANES]
            for t in range(2):
                c_out[m, t] = f_part[m, 2 * t + 1 - core].astype(BF16)
            send(c_out.at[m], c_in.at[m], c_s.at[m], c_r.at[m], core_other)
        if m >= 1:
            arrived(c_in.at[m - 1], c_r.at[m - 1])
            z_out[m - 1] = (
                f_part[m - 1, 2 * (1 - mine) + core] + c_in[m - 1, 1 - mine].astype(F32)
            ).astype(BF16)
            send(z_out.at[m - 1], z_in.at[m - 1], z_s.at[m - 1], z_r.at[m - 1], zl_other)
    a_next = a_all.at[2 * (1 - zl) + core]
    arrived(a_next, a_r.at[0])
    send(a_next, a_next, a_s.at[2], a_r.at[2], core_other)
    for m in range(4):
        arrived(z_in.at[m], z_r.at[m])
        h_all[y, pl.ds(m * HALF, HALF)] = (
            f_part[m, 2 * mine + core] + c_in[m, mine].astype(F32) + z_in[m].astype(F32)
        ).astype(BF16)
        for way in range(2):
            ring_send(h_all, h_s, h_r, way, 0, m)
    ring_hop(h_all, h_s, h_r, 1, AS_MADE[:2])
    arrived(a_all.at[2 * zl + 1 - core], a_r.at[1])
    arrived(a_all.at[2 * (1 - zl) + 1 - core], a_r.at[2])

    order = rem(y, 4)
    last = jnp.where(order == 0, 3, jnp.where(order == 3, 4, 5))
    steps = (
        (0,),
        (7, 1),
        (6, 2),
        (jnp.where(order == 0, 4, jnp.where(order == 3, 5, 3)), jnp.where(order == 0, 5, jnp.where(order == 3, 3, 4))),
        (last,),
    )

    def owner_x(o, plane):
        yy = rem(y + o, RY)
        return 2 * rem(plane + yy, 2) + div(yy, 4)

    def rows_at(o, at_x):
        away = rem(at_x + RX - owner_x(o, zl), RX)
        return 2 * (1 - rem(away, 2)) + div(away, 2)

    def multiply(step, s):
        offsets = steps[step]
        right = jnp.concatenate([h_all[rem(y + o, RY)] for o in offsets], axis=1)
        product = jnp.dot(a_all[s], right, preferred_element_type=F32).astype(BF16)
        for i, o in enumerate(offsets):
            to_x = rem(owner_x(o, zl) + 2 * rem(s, 2) + 1 - div(s, 2), RX)
            for half in range(2):
                part[step, to_x, half, i] = product[half * HALF : (half + 1) * HALF, i * LANES : (i + 1) * LANES]

    def count(step):
        return pl.ds(0, len(SLOTS[step]))

    s_up, s_down, s_far = rem(x + 1, RX), rem(x + RX - 1, RX), rem(x + 2, RX)

    def x_send(step):
        n = count(step)
        s_first = rows_at(steps[step][0], s_far)
        s_next = rows_at(steps[step][-1], s_far)
        s_next = jnp.where(s_next == s_first, rows_at(steps[step][0], s_down), s_next)
        s_third = rem(s_first + 1, 4)
        s_third = jnp.where(s_third == s_next, rem(s_first + 2, 4), s_third)
        rows = (s_first, s_next, s_third, 6 - s_first - s_next - s_third)
        early = len(SLOTS[step])
        for s in rows[:early]:
            multiply(step, s)
        send(part.at[step, s_far, 0, n], relayed.at[step, 0, n], x_s.at[step, 0], rel_r.at[step, 0], x_down)
        send(part.at[step, s_far, 1, n], relayed.at[step, 1, n], x_s.at[step, 1], rel_r.at[step, 1], x_up)
        for s in rows[early:]:
            multiply(step, s)
        send(part.at[step, s_down, 1, n], x_in.at[step, 0, 1, n], x_s.at[step, 2], x_r.at[step, 0, 1], x_down)
        send(part.at[step, s_up, 0, n], x_in.at[step, 1, 0, n], x_s.at[step, 3], x_r.at[step, 1, 0], x_up)

    def x_relay(step):
        n = count(step)
        for half, s, to in ((0, s_down, x_down), (1, s_up, x_up)):
            arrived(relayed.at[step, half, n], rel_r.at[step, half])
            for i in range(len(SLOTS[step])):
                part[step, s, half, i] = (
                    part[step, s, half, i].astype(F32) + relayed[step, half, i].astype(F32)
                ).astype(BF16)
            send(
                part.at[step, s, half, n], x_in.at[step, half, half, n], x_s.at[step, 4 + half],
                x_r.at[step, half, half], to,
            )

    def z_send(step):
        n = count(step)
        for half in range(2):
            for side in range(2):
                arrived(x_in.at[step, side, half, n], x_r.at[step, side, half])
            for i in range(len(SLOTS[step])):
                total = (
                    part[step, x, half, i].astype(F32)
                    + x_in[step, 0, half, i].astype(F32)
                    + x_in[step, 1, half, i].astype(F32)
                ).astype(BF16)
                for q in range(2):
                    x_sum[step, 2 * half + q, i] = total[q * QUARTER : (q + 1) * QUARTER]
            for q in range(2 * half, 2 * half + 2):
                send(
                    x_sum.at[step, q, n], z_part.at[step, zh, n], zz_s.at[step, q], zz_r.at[step, zh],
                    device(zl_=1 - zl, zh_=jnp.int32(q)),
                )

    def owner(o):
        to_x = owner_x(o, 1 - zl)
        away = rem(x + RX - to_x, RX)
        return 1 - rem(away, 2), div(away, 2), to_x, rem(rem(y + o, RY), 4)

    def owned_here(o):
        to_zl, to_core, to_x, to_zh = owner(o)
        return (zl == to_zl) & (core == to_core) & (to_x == x) & (to_zh == zh)

    def piece(half, q):
        return out_ref.at[pl.ds(q * QUARTER, QUARTER), pl.ds(pl.multiple_of(half * LANES, LANES), LANES)]

    def last_send(step):
        n = count(step)
        for s in range(RZ):
            arrived(z_part.at[step, s, n], zz_r.at[step, s])
        for i, (slot, o) in enumerate(zip(SLOTS[step], steps[step])):
            total = z_part[step, 0, i].astype(F32)
            for s in range(1, RZ):
                total = total + z_part[step, s, i].astype(F32)
            z_sum[slot] = total.astype(BF16)
            to_zl, to_core, to_x, to_zh = owner(o)

            @pl.when(owned_here(o))
            def _():
                pltpu.make_async_copy(z_sum.at[slot], piece(core, zh), last_s.at[slot]).start()

            @pl.when(jnp.logical_not(owned_here(o)))
            def _():
                send(
                    z_sum.at[slot], piece(core, zh), last_s.at[slot], last_r.at[core, zh],
                    device(zl_=to_zl, core_=to_core, x_=to_x, zh_=to_zh),
                )

    def g_sent():
        for hop in range(4):
            ring_sent(g_all, g_s, hop)

    def b_sent():
        for e in NEAR_ZH:
            for h in range(2):

                def left_here():
                    sent(b_turned.at[h], bz_s.at[h, e])

                if e == 0:
                    pl.when(jnp.logical_not(b_source & (core == h)))(left_here)
                else:
                    left_here()

        for i in range(2 * RZ):
            sent(chunk(0, i), bp_s.at[i])

        @pl.when(b_source)
        def _():
            for i in range(2 * RZ):
                sent(chunk(0, i), bm_s.at[i])

    def a_sent():
        for i in range(3):
            sent(a_all.at[0], a_s.at[i])
        for m in range(4):
            sent(c_out.at[m], c_s.at[m])
            sent(z_out.at[m], z_s.at[m])
        ring_sent(h_all, h_s, 0)

    def steps_sent(step):
        n = count(step)
        for i in range(6):
            sent(part.at[step, 0, 0, n], x_s.at[step, i])
        for q in range(RZ):
            sent(x_sum.at[step, q, n], zz_s.at[step, q])

    def all_sent(step):
        if step == 0:
            g_sent()
        elif step == 1:
            b_sent()
        elif step == 2:
            a_sent()
        else:
            ring_sent(h_all, h_s, step - 2)
            steps_sent(step - 3)

    for step in range(len(SLOTS) + 2):
        if step == 3:
            ring_end(h_all, h_r)
        if step < len(SLOTS):
            x_send(step)
            if step < 3:
                ring_hop(h_all, h_s, h_r, step + 1, AS_MADE[2 if step == 0 else 0 :])
            all_sent(step)
            x_relay(step)
        for stage, back in ((z_send, 1), (last_send, 2)):
            if 0 <= step - back < len(SLOTS):
                stage(step - back)
        if step == 5:
            steps_sent(2)

    ring_sent(h_all, h_s, 3)
    steps_sent(3)
    steps_sent(4)
    for slot, o in enumerate(o for offsets in steps for o in offsets):

        @pl.when(owned_here(o))
        def _():
            pltpu.make_async_copy(z_sum.at[slot], piece(core, zh), last_s.at[slot]).wait()

        @pl.when(jnp.logical_not(owned_here(o)))
        def _():
            sent(z_sum.at[slot], last_s.at[slot])

    for half in range(2):
        for q in range(RZ):

            @pl.when(jnp.logical_not(from_here(half, q)))
            def _():
                arrived(piece(jnp.int32(half), jnp.int32(q)), last_r.at[half, q])


def body(out_inverse, gradient, in_inverse):
    dma = pltpu.SemaphoreType.DMA
    vmem = pltpu.VMEM
    return pl.pallas_call(
        kernel,
        out_shape=jax.ShapeDtypeStruct((ROWS, 2 * LANES), BF16),
        in_specs=[pl.BlockSpec(memory_space=pl.ANY)] * 3,
        out_specs=pl.BlockSpec(memory_space=pl.ANY),
        scratch_shapes=[
            vmem((4, ROWS, 2 * ROWS), BF16),
            vmem((RY, 2 * ROWS, LANES), BF16),
            vmem((2, LANES, LANES), BF16),
            vmem((2, LANES, LANES), BF16),
            vmem((RY, 4, LANES, LANES), BF16),
            vmem((4, 4, HALF, LANES), F32),
            vmem((4, 2, HALF, LANES), BF16),
            vmem((4, 2, HALF, LANES), BF16),
            vmem((4, HALF, LANES), BF16),
            vmem((4, HALF, LANES), BF16),
            vmem((RY, 2 * ROWS, LANES), BF16),
            vmem((5, 4, 2, 2, HALF, LANES), BF16),
            vmem((5, 2, 2, HALF, LANES), BF16),
            vmem((5, 2, 2, 2, HALF, LANES), BF16),
            vmem((5, RZ, 2, QUARTER, LANES), BF16),
            vmem((5, RZ, 2, QUARTER, LANES), BF16),
            vmem((RY, QUARTER, LANES), BF16),
            dma((4,)),
            dma((2, 4, 4)), dma((2, 4, 4)),
            dma((2, 4, 4)), dma((2, 4, 4)),
            dma((2, RZ)), dma((4, RZ)),
            dma((2 * RZ,)), dma((2 * RZ,)),
            dma((2 * RZ,)), dma((2 * RZ,)),
            dma((3,)), dma((3,)),
            dma((4,)), dma((4,)),
            dma((4,)), dma((4,)),
            dma((5, 6)), dma((5, 2)), dma((5, 2, 2)),
            dma((5, RZ)), dma((5, RZ)),
            dma((RY,)), dma((2, RZ)),
        ],
        compiler_params=pltpu.CompilerParams(
            collective_id=0, has_side_effects=True, vmem_limit_bytes=64 * 1024 * 1024
        ),
        cost_estimate=pl.CostEstimate(flops=4_300_000_000, bytes_accessed=2_000_000, transcendentals=0),
    )(out_inverse, gradient, in_inverse)


def solution(mesh):
    in_specs = (P("row", "col"), P("col", "row"), P("row", "col"))
    return jax.shard_map(body, mesh=mesh, in_specs=in_specs, out_specs=P("row", "col"), check_vma=False)
```

```python
import jax
import jax.numpy as jnp
from jax import lax
from jax.experimental import pallas as pl
from jax.experimental.pallas import tpu as pltpu
from jax.sharding import PartitionSpec as P

MESH = pl.DeviceIdType.MESH
BF16 = jnp.bfloat16
F32 = jnp.float32
RY, RX, RZ = 8, 4, 4
ROWS, HALF, QUARTER, LANES = 448, 224, 112, 128
SLOTS = ((0,), (1, 2), (3, 4), (5, 6), (7,))
NEAR_Z = (0, 1, 7, 2, 6, 3, 5, 4)
NEAR_ZH = (0, 1, 3, 2)
FAR_FIRST = ((0, 0), (1, 2), (0, 1), (1, 3), (0, 2), (1, 0), (0, 3), (1, 1))
AS_MADE = ((0, 0), (1, 0), (0, 1), (1, 1), (0, 2), (1, 2), (0, 3), (1, 3))


def rem(a, b):
    return lax.rem(a, jnp.int32(b))


def div(a, b):
    return lax.div(a, jnp.int32(b))


def kernel(
    a_ref, g_ref, b_ref, out_ref,
    a_all, g_all, b_own, b_turned, b_all, f_part, c_out, c_in, z_out, z_in, h_all, part, relayed, x_in, x_sum, z_part, z_sum,
    loc, g_s, g_r, h_s, h_r, bz_s, bz_r, bm_s, bm_r, bp_s, bp_r, a_s, a_r, c_s, c_r, z_s, z_r,
    x_s, rel_r, x_r, zz_s, zz_r, last_s, last_r,
):
    row, col = lax.axis_index("row"), lax.axis_index("col")
    core = rem(row, 2)
    y = rem(div(row, 2), RY)
    zl = div(row, 2 * RY)
    x, zh = div(col, RZ), rem(col, RZ)
    own = zl * 2 + core

    def device(zl_=zl, y_=y, core_=core, x_=x, zh_=zh):
        return ((zl_ * RY + y_) * 2 + core_, x_ * RZ + zh_)

    y_to = (device(y_=rem(y + 1, RY)), device(y_=rem(y + RY - 1, RY)))
    x_up, x_down = device(x_=rem(x + 1, RX)), device(x_=rem(x + RX - 1, RX))
    core_other, zl_other = device(core_=1 - core), device(zl_=1 - zl)
    x_pair, x_mirror = device(x_=x + 1 - 2 * rem(x, 2)), device(x_=RX - 1 - x)

    def remote(src, dst, send, recv, to):
        return pltpu.make_async_remote_copy(
            src_ref=src, dst_ref=dst, send_sem=send, recv_sem=recv, device_id=to, device_id_type=MESH
        )

    def send(src, dst, s, r, to):
        remote(src, dst, s, r, to).start()

    def sent(src, s):
        remote(src, src, s, s, core_other).wait_send()

    def arrived(dst, r):
        remote(dst, dst, r, r, core_other).wait_recv()

    loads = [
        pltpu.make_async_copy(g_ref, g_all.at[y], loc.at[0]),
        pltpu.make_async_copy(b_ref.at[:, pl.ds(0, LANES)], b_own.at[0], loc.at[1]),
        pltpu.make_async_copy(b_ref.at[:, pl.ds(LANES, LANES)], b_own.at[1], loc.at[2]),
        pltpu.make_async_copy(a_ref, a_all.at[own], loc.at[3]),
    ]
    for load in loads:
        load.start()
    barrier = pltpu.get_barrier_semaphore()
    for to in (*y_to, x_up, x_down):
        pl.semaphore_signal(barrier, inc=1, device_id=to, device_id_type=MESH)
    place = (zh * 2 + zl) * 2 + core
    for step in range(1, 16):
        there = rem(place + step, 16)
        pl.semaphore_signal(
            barrier,
            inc=1,
            device_id=device(zl_=rem(div(there, 2), 2), core_=rem(there, 2), zh_=div(there, 4)),
            device_id_type=MESH,
        )
    from_zl = 1 - rem(div(x, 2) + rem(zh, 2), 2)
    from_x = rem(x + 2 * core + 1 - zl, RX)

    def from_here(half, q):
        return (x == from_x) & (zl == from_zl) & (core == half) & (zh == q)

    for half in range(2):
        for q in range(RZ):

            @pl.when(jnp.logical_not(from_here(half, q)))
            def _():
                pl.semaphore_signal(
                    barrier,
                    inc=1,
                    device_id=device(zl_=from_zl, core_=jnp.int32(half), x_=from_x, zh_=jnp.int32(q)),
                    device_id_type=MESH,
                )

    for load in loads:
        load.wait()
    for h in range(2):
        b_turned[h] = b_own[h].astype(F32).T.astype(BF16)
    pl.semaphore_wait(barrier, 27 - jnp.where((x == from_x) & (zl == from_zl), 1, 0))

    def ring_part(buf, owner, i):
        return buf.at[owner, pl.ds(i * HALF, HALF)]

    def ring_send(buf, s, r, way, hop, i):
        owner = rem(y + (RY - hop if way == 0 else hop), RY)
        send(ring_part(buf, owner, i), ring_part(buf, owner, i), s.at[way, hop, i], r.at[way, hop, i], y_to[way])

    def ring_wait(buf, r, way, hop, i):
        owner = rem(y + (RY - hop - 1 if way == 0 else hop + 1), RY)
        arrived(ring_part(buf, owner, i), r.at[way, hop, i])

    def ring_hop(buf, s, r, hop, parts=FAR_FIRST):
        for way, i in parts:
            ring_wait(buf, r, way, hop - 1, i)
            if hop < 3 or i // 2 == way:
                ring_send(buf, s, r, way, hop, i)

    def ring_end(buf, r):
        for way, i in FAR_FIRST:
            if i // 2 == way:
                ring_wait(buf, r, way, 3, i)

    def ring_sent(buf, s, hop):
        for way, i in FAR_FIRST:
            if hop < 3 or i // 2 == way:
                sent(ring_part(buf, 0, i), s.at[way, hop, i])

    for way, i in FAR_FIRST:
        ring_send(g_all, g_s, g_r, way, 0, i)

    b_here = rem(x, 2) * 4
    b_zl = div(x, 2)

    b_source = zl == b_zl
    b_first = rem(rem(x, 2) + rem(b_zl + zl, 2), 2) * 4

    for e in NEAR_ZH:
        to_zh = rem(zh + e, RZ)
        for h in range(2):

            def away():
                send(
                    b_turned.at[h], b_all.at[b_here + zh, own], bz_s.at[h, e], bz_r.at[own, zh],
                    device(zl_=b_zl, core_=jnp.int32(h), zh_=to_zh),
                )

            if e == 0:

                @pl.when(b_source & (core == h))
                def _():
                    b_all[b_here + zh, own] = b_turned[h]

                pl.when(jnp.logical_not(b_source & (core == h)))(away)
            else:
                away()

    def chunk(half, i):
        there = rem(2 * zh + zl + NEAR_Z[i], 2 * RZ)
        return b_all.at[half + div(there, 2), pl.ds(2 * rem(there, 2), 2)]

    def b_start(first, last):
        @pl.when(b_source)
        def _():
            for i in range(first, last):
                there = rem(2 * zh + zl + NEAR_Z[i], 2 * RZ)
                for c in range(2) if i > 0 else (1 - core,):
                    s = 2 * rem(there, 2) + c
                    arrived(b_all.at[b_here + div(there, 2), s], bz_r.at[s, div(there, 2)])
                block = chunk(b_here, i)
                send(block, block, bm_s.at[i], bm_r.at[i], x_mirror)
                send(block, block, bp_s.at[i], bp_r.at[i], x_pair)

    def b_forward(first, last):
        @pl.when(jnp.logical_not(b_source))
        def _():
            for i in range(first, last):
                block = chunk(b_first, i)
                arrived(block, bm_r.at[i])
                send(block, block, bp_s.at[i], bp_r.at[i], x_pair)

    b_start(0, 3)
    ring_hop(g_all, g_s, g_r, 1)
    b_start(3, 8)
    send(a_all.at[own], a_all.at[own], a_s.at[0], a_r.at[0], zl_other)
    send(a_all.at[own], a_all.at[own], a_s.at[1], a_r.at[1], core_other)
    b_forward(0, 3)
    ring_hop(g_all, g_s, g_r, 2)
    b_forward(3, 8)
    ring_hop(g_all, g_s, g_r, 3)
    ring_end(g_all, g_r)
    for i in range(2 * RZ):
        arrived(chunk(4 - b_first, i), bp_r.at[i])

    mine = rem(zl + y, 2)
    right = jnp.concatenate([b_all[:, t].reshape(RY * LANES, LANES) for t in range(4)], axis=1)
    for m in range(5):
        if m < 4:
            rows = pl.ds(m * HALF, HALF)
            left = jnp.concatenate([g_all[j, rows] for j in range(RY)], axis=1)
            share = jnp.dot(left, right, preferred_element_type=F32)
            for t in range(4):
                f_part[m, t] = share[:, t * LANES : (t + 1) * LANES]
            for t in range(2):
                c_out[m, t] = f_part[m, 2 * t + 1 - core].astype(BF16)
            send(c_out.at[m], c_in.at[m], c_s.at[m], c_r.at[m], core_other)
        if m >= 1:
            arrived(c_in.at[m - 1], c_r.at[m - 1])
            z_out[m - 1] = (
                f_part[m - 1, 2 * (1 - mine) + core] + c_in[m - 1, 1 - mine].astype(F32)
            ).astype(BF16)
            send(z_out.at[m - 1], z_in.at[m - 1], z_s.at[m - 1], z_r.at[m - 1], zl_other)
    a_next = a_all.at[2 * (1 - zl) + core]
    arrived(a_next, a_r.at[0])
    send(a_next, a_next, a_s.at[2], a_r.at[2], core_other)
    for m in range(4):
        arrived(z_in.at[m], z_r.at[m])
        h_all[y, pl.ds(m * HALF, HALF)] = (
            f_part[m, 2 * mine + core] + c_in[m, mine].astype(F32) + z_in[m].astype(F32)
        ).astype(BF16)
        for way in range(2):
            ring_send(h_all, h_s, h_r, way, 0, m)
    ring_hop(h_all, h_s, h_r, 1, AS_MADE[:2])
    arrived(a_all.at[2 * zl + 1 - core], a_r.at[1])
    arrived(a_all.at[2 * (1 - zl) + 1 - core], a_r.at[2])

    order = rem(y, 4)
    last = jnp.where(order == 0, 3, jnp.where(order == 3, 4, 5))
    steps = (
        (0,),
        (7, 1),
        (6, 2),
        (jnp.where(order == 0, 4, jnp.where(order == 3, 5, 3)), jnp.where(order == 0, 5, jnp.where(order == 3, 3, 4))),
        (last,),
    )

    def owner_x(o, plane):
        yy = rem(y + o, RY)
        return 2 * rem(plane + yy, 2) + div(yy, 4)

    def rows_at(o, at_x):
        away = rem(at_x + RX - owner_x(o, zl), RX)
        return 2 * (1 - rem(away, 2)) + div(away, 2)

    def multiply(step, s):
        offsets = steps[step]
        right = jnp.concatenate([h_all[rem(y + o, RY)] for o in offsets], axis=1)
        product = jnp.dot(a_all[s], right, preferred_element_type=F32).astype(BF16)
        for i, o in enumerate(offsets):
            to_x = rem(owner_x(o, zl) + 2 * rem(s, 2) + 1 - div(s, 2), RX)
            for half in range(2):
                part[step, to_x, half, i] = product[half * HALF : (half + 1) * HALF, i * LANES : (i + 1) * LANES]

    def count(step):
        return pl.ds(0, len(SLOTS[step]))

    s_up, s_down, s_far = rem(x + 1, RX), rem(x + RX - 1, RX), rem(x + 2, RX)

    def x_send(step):
        n = count(step)
        s_first = rows_at(steps[step][0], s_far)
        s_next = rows_at(steps[step][-1], s_far)
        s_next = jnp.where(s_next == s_first, rows_at(steps[step][0], s_down), s_next)
        s_third = rem(s_first + 1, 4)
        s_third = jnp.where(s_third == s_next, rem(s_first + 2, 4), s_third)
        rows = (s_first, s_next, s_third, 6 - s_first - s_next - s_third)
        early, late = len(SLOTS[step]), 4
        if early == 1:
            rows, late = tuple(rows_at(steps[step][0], to_x) for to_x in (s_far, s_down, s_up, x)), 3
        for s in rows[:early]:
            multiply(step, s)
        send(part.at[step, s_far, 0, n], relayed.at[step, 0, n], x_s.at[step, 0], rel_r.at[step, 0], x_down)
        send(part.at[step, s_far, 1, n], relayed.at[step, 1, n], x_s.at[step, 1], rel_r.at[step, 1], x_up)
        for s in rows[early:late]:
            multiply(step, s)
        send(part.at[step, s_down, 1, n], x_in.at[step, 0, 1, n], x_s.at[step, 2], x_r.at[step, 0, 1], x_down)
        send(part.at[step, s_up, 0, n], x_in.at[step, 1, 0, n], x_s.at[step, 3], x_r.at[step, 1, 0], x_up)
        for s in rows[late:]:
            multiply(step, s)

    def x_relay(step):
        n = count(step)
        for half, s, to in ((0, s_down, x_down), (1, s_up, x_up)):
            arrived(relayed.at[step, half, n], rel_r.at[step, half])
            for i in range(len(SLOTS[step])):
                part[step, s, half, i] = (
                    part[step, s, half, i].astype(F32) + relayed[step, half, i].astype(F32)
                ).astype(BF16)
            send(
                part.at[step, s, half, n], x_in.at[step, half, half, n], x_s.at[step, 4 + half],
                x_r.at[step, half, half], to,
            )

    def z_send(step):
        n = count(step)
        for half in range(2):
            for side in range(2):
                arrived(x_in.at[step, side, half, n], x_r.at[step, side, half])
            for i in range(len(SLOTS[step])):
                total = (
                    part[step, x, half, i].astype(F32)
                    + x_in[step, 0, half, i].astype(F32)
                    + x_in[step, 1, half, i].astype(F32)
                ).astype(BF16)
                for q in range(2):
                    x_sum[step, 2 * half + q, i] = total[q * QUARTER : (q + 1) * QUARTER]
            for q in range(2 * half, 2 * half + 2):
                send(
                    x_sum.at[step, q, n], z_part.at[step, zh, n], zz_s.at[step, q], zz_r.at[step, zh],
                    device(zl_=1 - zl, zh_=jnp.int32(q)),
                )

    def owner(o):
        to_x = owner_x(o, 1 - zl)
        away = rem(x + RX - to_x, RX)
        return 1 - rem(away, 2), div(away, 2), to_x, rem(rem(y + o, RY), 4)

    def owned_here(o):
        to_zl, to_core, to_x, to_zh = owner(o)
        return (zl == to_zl) & (core == to_core) & (to_x == x) & (to_zh == zh)

    def piece(half, q):
        return out_ref.at[pl.ds(q * QUARTER, QUARTER), pl.ds(pl.multiple_of(half * LANES, LANES), LANES)]

    def last_send(step):
        n = count(step)
        for s in range(RZ):
            arrived(z_part.at[step, s, n], zz_r.at[step, s])
        for i, (slot, o) in enumerate(zip(SLOTS[step], steps[step])):
            total = z_part[step, 0, i].astype(F32)
            for s in range(1, RZ):
                total = total + z_part[step, s, i].astype(F32)
            z_sum[slot] = total.astype(BF16)
            to_zl, to_core, to_x, to_zh = owner(o)

            @pl.when(owned_here(o))
            def _():
                pltpu.make_async_copy(z_sum.at[slot], piece(core, zh), last_s.at[slot]).start()

            @pl.when(jnp.logical_not(owned_here(o)))
            def _():
                send(
                    z_sum.at[slot], piece(core, zh), last_s.at[slot], last_r.at[core, zh],
                    device(zl_=to_zl, core_=to_core, x_=to_x, zh_=to_zh),
                )

    def g_sent():
        for hop in range(4):
            ring_sent(g_all, g_s, hop)

    def b_sent():
        for e in NEAR_ZH:
            for h in range(2):

                def left_here():
                    sent(b_turned.at[h], bz_s.at[h, e])

                if e == 0:
                    pl.when(jnp.logical_not(b_source & (core == h)))(left_here)
                else:
                    left_here()

        for i in range(2 * RZ):
            sent(chunk(0, i), bp_s.at[i])

        @pl.when(b_source)
        def _():
            for i in range(2 * RZ):
                sent(chunk(0, i), bm_s.at[i])

    def a_sent():
        for i in range(3):
            sent(a_all.at[0], a_s.at[i])
        for m in range(4):
            sent(c_out.at[m], c_s.at[m])
            sent(z_out.at[m], z_s.at[m])
        ring_sent(h_all, h_s, 0)

    def steps_sent(step):
        n = count(step)
        for i in range(6):
            sent(part.at[step, 0, 0, n], x_s.at[step, i])
        for q in range(RZ):
            sent(x_sum.at[step, q, n], zz_s.at[step, q])

    def all_sent(step):
        if step == 0:
            g_sent()
        elif step == 1:
            b_sent()
        elif step == 2:
            a_sent()
        else:
            ring_sent(h_all, h_s, step - 2)
            steps_sent(step - 3)

    for step in range(len(SLOTS) + 2):
        if step == 3:
            ring_end(h_all, h_r)
        if step < len(SLOTS):
            x_send(step)
            if step < 3:
                ring_hop(h_all, h_s, h_r, step + 1, AS_MADE[2 if step == 0 else 0 :])
            all_sent(step)
            x_relay(step)
        for stage, back in ((z_send, 1), (last_send, 2)):
            if 0 <= step - back < len(SLOTS):
                stage(step - back)
        if step == 5:
            steps_sent(2)

    ring_sent(h_all, h_s, 3)
    steps_sent(3)
    steps_sent(4)
    for slot, o in enumerate(o for offsets in steps for o in offsets):

        @pl.when(owned_here(o))
        def _():
            pltpu.make_async_copy(z_sum.at[slot], piece(core, zh), last_s.at[slot]).wait()

        @pl.when(jnp.logical_not(owned_here(o)))
        def _():
            sent(z_sum.at[slot], last_s.at[slot])

    for half in range(2):
        for q in range(RZ):

            @pl.when(jnp.logical_not(from_here(half, q)))
            def _():
                arrived(piece(jnp.int32(half), jnp.int32(q)), last_r.at[half, q])


def body(out_inverse, gradient, in_inverse):
    dma = pltpu.SemaphoreType.DMA
    vmem = pltpu.VMEM
    return pl.pallas_call(
        kernel,
        out_shape=jax.ShapeDtypeStruct((ROWS, 2 * LANES), BF16),
        in_specs=[pl.BlockSpec(memory_space=pl.ANY)] * 3,
        out_specs=pl.BlockSpec(memory_space=pl.ANY),
        scratch_shapes=[
            vmem((4, ROWS, 2 * ROWS), BF16),
            vmem((RY, 2 * ROWS, LANES), BF16),
            vmem((2, LANES, LANES), BF16),
            vmem((2, LANES, LANES), BF16),
            vmem((RY, 4, LANES, LANES), BF16),
            vmem((4, 4, HALF, LANES), F32),
            vmem((4, 2, HALF, LANES), BF16),
            vmem((4, 2, HALF, LANES), BF16),
            vmem((4, HALF, LANES), BF16),
            vmem((4, HALF, LANES), BF16),
            vmem((RY, 2 * ROWS, LANES), BF16),
            vmem((5, 4, 2, 2, HALF, LANES), BF16),
            vmem((5, 2, 2, HALF, LANES), BF16),
            vmem((5, 2, 2, 2, HALF, LANES), BF16),
            vmem((5, RZ, 2, QUARTER, LANES), BF16),
            vmem((5, RZ, 2, QUARTER, LANES), BF16),
            vmem((RY, QUARTER, LANES), BF16),
            dma((4,)),
            dma((2, 4, 4)), dma((2, 4, 4)),
            dma((2, 4, 4)), dma((2, 4, 4)),
            dma((2, RZ)), dma((4, RZ)),
            dma((2 * RZ,)), dma((2 * RZ,)),
            dma((2 * RZ,)), dma((2 * RZ,)),
            dma((3,)), dma((3,)),
            dma((4,)), dma((4,)),
            dma((4,)), dma((4,)),
            dma((5, 6)), dma((5, 2)), dma((5, 2, 2)),
            dma((5, RZ)), dma((5, RZ)),
            dma((RY,)), dma((2, RZ)),
        ],
        compiler_params=pltpu.CompilerParams(
            collective_id=0, has_side_effects=True, vmem_limit_bytes=64 * 1024 * 1024
        ),
        cost_estimate=pl.CostEstimate(flops=4_300_000_000, bytes_accessed=2_000_000, transcendentals=0),
    )(out_inverse, gradient, in_inverse)


def solution(mesh):
    in_specs = (P("row", "col"), P("col", "row"), P("row", "col"))
    return jax.shard_map(body, mesh=mesh, in_specs=in_specs, out_specs=P("row", "col"), check_vma=False)
```
